32 devices in a mesh: seq: 8 (over z, core), head: 4 (over y, x).
Axes of the slice: x: 2, y: 2, z: 4, core: 2. Of those that a mesh axis runs over, the one named last changes fastest.
Arguments:
- queries: bfloat16 [2048, 2048], P('seq', 'head'), may hold values from -6 to 6
- key_states: bfloat16 [2048, 256], P('seq', 'head'), may hold values from -6 to 6
- value_states: bfloat16 [2048, 256], P('seq', 'head'), may hold values from -6 to 6
- block_picks: int32 [4, 2, 2], replicated, may hold values from 1 to 3, as said below
- grad_output: bfloat16 [2048, 2048], P('seq', 'head'), may hold values from -6 to 6
Outputs:
- attn_output: bfloat16 [2048, 2048], P('seq', 'head')
- grad_queries: float32 [2048, 2048], P('seq', 'head')
- grad_keys: float32 [2048, 256], P('seq', 'head')
- grad_values: float32 [2048, 256], P('seq', 'head')
The draws below stay inside these ranges and needn't reach their ends.
Inputs may be any that keep to these rules, and one draw needn't show every extreme that they name: `block_picks`: for query block b and KV head g the offsets differ from each other and lie in 1 to max(b, 2).
All inputs are finite; a program needn't handle non-finite values.
Results may differ from the reference program's by a relative error of at most 0.0095.
Values may be sent and summed in bfloat16 or wider, within the bound.
A program may use at most 64 MiB of HBM per device.

```python
import jax
import jax.numpy as jnp
from jax import lax

HEAD_DIM = 128
BLOCK = 512
QH = 16
KVH = 2
SEQ = 2048
NBLK = 4


def draw_queries(key, part):
    draws_base = jnp.clip(jax.random.normal(jax.random.fold_in(key, 1), (SEQ, QH, HEAD_DIM), jnp.float32), -6.0, 6.0)
    return draws_base.reshape(SEQ, QH * HEAD_DIM).astype(jnp.bfloat16)


def draw_key_states(key, part):
    draws_base = jnp.clip(jax.random.normal(jax.random.fold_in(key, 2), (SEQ, KVH, HEAD_DIM), jnp.float32), -6.0, 6.0)
    return draws_base.reshape(SEQ, KVH * HEAD_DIM).astype(jnp.bfloat16)


def draw_block_picks(key, part):
    block_index = jnp.arange(NBLK, dtype=jnp.int32)[:, None]
    reach_max = jnp.maximum(block_index, 2)
    first_pick = jax.random.randint(jax.random.fold_in(key, 3), (NBLK, KVH), 0, 1 << 20, jnp.int32) % reach_max
    last_row = (block_index == NBLK - 1) & (jnp.arange(KVH, dtype=jnp.int32)[None, :] == 0)
    first_pick = jnp.where(last_row, reach_max - 1, first_pick)
    second = jax.random.randint(jax.random.fold_in(key, 4), (NBLK, KVH), 0, 1 << 20, jnp.int32) % (reach_max - 1)
    offset_one = 1 + first_pick
    offset_two = 1 + (first_pick + 1 + second) % reach_max
    return jnp.stack([offset_one, offset_two], -1).astype(jnp.int32)


def steps_of(key, dims, cuts, smallest, top_value):
    gain = 1.0
    for dim, parts in cuts:
        heights = jax.random.uniform(jax.random.fold_in(jax.random.fold_in(key, 6), dim), (parts,), jnp.float32, smallest / len(cuts), top_value / len(cuts))
        gain = gain * jnp.repeat(jnp.exp(heights), dims[dim] // parts).reshape((-1,) + (1,) * (len(dims) - 1 - dim))
    return gain


def normal_values(rng, dims, spread, reach, cuts=(), held_as=jnp.bfloat16):
    entries = spread * jax.random.normal(rng, dims, jnp.float32)
    if cuts:
        entries = entries * steps_of(rng, dims, cuts, -0.22, 0.18)
    return jnp.clip(entries, -reach, reach).astype(held_as)


def setup_inputs(seed: int = 0) -> dict:
    splits = jax.random.split(jax.random.key(seed), 6)
    return {
        "queries": draw_queries(jax.random.fold_in(splits[5], 71), 0),
        "key_states": draw_key_states(jax.random.fold_in(splits[5], 71), 0),
        "value_states": normal_values(splits[2], (SEQ, KVH * HEAD_DIM), 1.0, 6.0, ((0, 8), (1, 4))),
        "block_picks": draw_block_picks(jax.random.fold_in(splits[5], 71), 0),
        "grad_output": normal_values(splits[4], (SEQ, QH * HEAD_DIM), 1.0, 6.0, ((0, 8), (1, 4))),
    }


NEGATIVE = -1.0e30


def reference(queries, key_states, value_states, block_picks, grad_output):
    seq_len = queries.shape[0]
    num_blocks = seq_len // BLOCK
    kv_heads = key_states.shape[1] // HEAD_DIM
    group_size = queries.shape[1] // key_states.shape[1]
    chosen = block_picks.shape[2] + 1
    scaling = HEAD_DIM ** -0.5
    query_cube = queries.reshape(num_blocks, BLOCK, kv_heads, group_size, HEAD_DIM)
    grad_cube = grad_output.reshape(num_blocks, BLOCK, kv_heads, group_size, HEAD_DIM)
    key_cube = key_states.reshape(num_blocks, BLOCK, kv_heads, HEAD_DIM)
    value_cube = value_states.reshape(num_blocks, BLOCK, kv_heads, HEAD_DIM)
    key_count = chosen * BLOCK
    positions = jnp.arange(BLOCK, dtype=jnp.int32)
    slot_index = jnp.arange(key_count, dtype=jnp.int32) // BLOCK
    key_place = jnp.arange(key_count, dtype=jnp.int32) % BLOCK

    def advance(totals, item_index):
        grad_key_acc, grad_value_acc = totals
        block_index = (item_index // kv_heads).astype(jnp.int32)
        head_index = (item_index % kv_heads).astype(jnp.int32)
        zero = jnp.zeros((), jnp.int32)
        q_rows = lax.dynamic_slice(query_cube, (block_index, zero, head_index, zero, zero), (1, BLOCK, 1, group_size, HEAD_DIM))
        q_rows = q_rows.reshape(BLOCK, group_size, HEAD_DIM).astype(jnp.float32)
        g_rows = lax.dynamic_slice(grad_cube, (block_index, zero, head_index, zero, zero), (1, BLOCK, 1, group_size, HEAD_DIM))
        g_rows = g_rows.reshape(BLOCK, group_size, HEAD_DIM).astype(jnp.float32)
        offsets = lax.dynamic_slice(block_picks, (block_index, head_index, zero), (1, 1, chosen - 1)).reshape(chosen - 1)
        selected = jnp.concatenate([block_index[None], block_index - offsets.astype(jnp.int32)])
        usable = selected >= 0
        block_ids = jnp.maximum(selected, 0).astype(jnp.int32)
        head_keys = lax.dynamic_index_in_dim(key_cube, head_index, 2, keepdims=False)
        head_values = lax.dynamic_index_in_dim(value_cube, head_index, 2, keepdims=False)
        key_tile = jnp.take(head_keys, block_ids, axis=0).reshape(key_count, HEAD_DIM).astype(jnp.float32)
        value_tile = jnp.take(head_values, block_ids, axis=0).reshape(key_count, HEAD_DIM).astype(jnp.float32)
        scores = jnp.einsum("rhd,kd->hrk", q_rows, key_tile) * scaling
        allowed = usable[slot_index][None, :] & ((slot_index[None, :] > 0) | (key_place[None, :] <= positions[:, None]))
        scores = jnp.where(allowed[None], scores, NEGATIVE)
        row_max = jnp.max(scores, axis=-1, keepdims=True)
        weights = jnp.exp(scores - row_max)
        probs = weights / jnp.sum(weights, axis=-1, keepdims=True)
        probs_low = lax.optimization_barrier(probs.astype(jnp.bfloat16)).astype(jnp.float32)
        attended = jnp.einsum("hrk,kd->rhd", probs_low, value_tile)
        row_delta = jnp.sum(g_rows * attended, axis=-1)
        grad_prob = jnp.einsum("rhd,kd->hrk", g_rows, value_tile)
        dscore = probs * (grad_prob - jnp.transpose(row_delta)[..., None])
        dscore = lax.optimization_barrier(dscore.astype(jnp.bfloat16)).astype(jnp.float32)
        grad_q = jnp.einsum("hrk,kd->rhd", dscore, key_tile) * scaling
        grad_k = jnp.einsum("hrk,rhd->kd", dscore, q_rows) * scaling
        grad_v = jnp.einsum("hrk,rhd->kd", probs_low, g_rows)
        grad_key_acc = grad_key_acc.at[head_index, block_ids].add(grad_k.reshape(chosen, BLOCK, HEAD_DIM))
        grad_value_acc = grad_value_acc.at[head_index, block_ids].add(grad_v.reshape(chosen, BLOCK, HEAD_DIM))
        return (grad_key_acc, grad_value_acc), (attended.astype(jnp.bfloat16), grad_q)

    start_acc = jnp.zeros((kv_heads, num_blocks, BLOCK, HEAD_DIM), jnp.float32)
    items = jnp.arange(num_blocks * kv_heads, dtype=jnp.int32)
    (grad_key_acc, grad_value_acc), (outputs, grad_qs) = lax.scan(advance, (start_acc, start_acc), items)
    attn_output = outputs.reshape(num_blocks, kv_heads, BLOCK, group_size, HEAD_DIM).transpose(0, 2, 1, 3, 4).reshape(seq_len, -1)
    grad_queries = grad_qs.reshape(num_blocks, kv_heads, BLOCK, group_size, HEAD_DIM).transpose(0, 2, 1, 3, 4).reshape(seq_len, -1)
    grad_keys = grad_key_acc.transpose(1, 2, 0, 3).reshape(seq_len, kv_heads * HEAD_DIM)
    grad_values = grad_value_acc.transpose(1, 2, 0, 3).reshape(seq_len, kv_heads * HEAD_DIM)
    return attn_output, grad_queries, grad_keys, grad_values
```

```python
import functools

import jax
import jax.numpy as jnp
from jax import lax
from jax.experimental import pallas as pl
from jax.experimental.pallas import tpu as pltpu
from jax.sharding import PartitionSpec as P

BLOCK = 512
NEGATIVE = -1e30
LOG2E = 1.4426950408889634
MESH = pl.DeviceIdType.MESH
F32 = jnp.float32
BF16 = jnp.bfloat16


def dot(a, b, contract):
    return lax.dot_general(a, b, ((contract[:1], contract[1:]), ((), ())), preferred_element_type=F32)


def kernel(
    seq_size, chosen, picks, k_in, v_in, q_hbm, g_hbm, attn_hbm, dq_hbm, dk_out, dv_out,
    kv, q4, g4, ev, dpv, p_low, ds_low, k_t, v_t, top, total, prod, attn_buf, dq_buf,
    part, core_in, x_out, x_in, summed, z_out, z_in,
    in_sem, out_sem, zs, zr, xs, xr, cs, cr, cs2, cr2, xs2, xr2, zs2, zr2,
):
    rows, half = k_in.shape
    dim = 2 * half
    heads = q4.shape[0]
    num_blocks = kv.shape[0]
    seq = lax.axis_index("seq")
    head = lax.axis_index("head")
    b, c = seq // 2, seq % 2
    x, group = head % 2, head // 2
    oc, ox = 1 - c, 1 - x
    core_dev = (2 * b + oc, head)
    x_dev = (seq, 2 * group + ox)
    scaling = dim ** (-0.5)
    rate = scaling * LOG2E

    def remote(src, dst, send, recv, dev):
        return pltpu.make_async_remote_copy(
            src_ref=src, dst_ref=dst, send_sem=send, recv_sem=recv, device_id=dev, device_id_type=MESH
        )

    loads = []
    for h in range(heads):
        cols = pl.ds(h * dim, dim)
        loads.append(pltpu.make_async_copy(q_hbm.at[:, cols], q4.at[h], in_sem.at[0, h]))
        loads.append(pltpu.make_async_copy(g_hbm.at[:, cols], g4.at[h], in_sem.at[1, h]))
    for load in loads:
        load.start()

    barrier = pltpu.get_barrier_semaphore()
    pl.semaphore_signal(barrier, inc=1, device_id=core_dev, device_id_type=MESH)
    pl.semaphore_signal(barrier, inc=1, device_id=x_dev, device_id_type=MESH)
    for d in range(1, num_blocks):
        other = lax.rem(b + d, num_blocks)
        pl.semaphore_signal(barrier, inc=1, device_id=(2 * other + c, head), device_id_type=MESH)
    kv[b, c, x] = jnp.concatenate([k_in[...], v_in[...]], axis=1)
    pl.semaphore_wait(barrier, num_blocks + 1)

    def z_gather(d):
        mine = kv.at[b, c, x]
        return remote(mine, mine, zs.at[d], zr.at[d], (2 * (b + d) + c, head))

    def z_arrival(d):
        piece = kv.at[b - d, c, x]
        return remote(piece, piece, zs.at[d], zr.at[d], (2 * (b - d) + c, head))

    def x_gather(d, side):
        piece = kv.at[b - d, c, side]
        return remote(piece, piece, xs.at[d], xr.at[d], x_dev)

    def core_gather(d, which, row_half):
        piece = kv.at[b - d, row_half, x if which == 0 else ox]
        return remote(piece, piece, cs.at[d, which], cr.at[d, which], core_dev)

    x_gather(0, x).start()
    for d in reversed(range(1, num_blocks)):
        @pl.when(b + d < num_blocks)
        def _():
            z_gather(d).start()
    core_gather(0, 0, c).start()

    def forward_z(d):
        @pl.when(d <= b)
        def _():
            z_arrival(d).wait_recv()
            x_gather(d, x).start()
            core_gather(d, 0, c).start()

    def forward_x(d):
        @pl.when(d <= b)
        def _():
            x_gather(d, ox).wait_recv()
            core_gather(d, 1, c).start()

    def settle(d):
        @pl.when(d <= b)
        def _():
            core_gather(d, 0, oc).wait_recv()
            core_gather(d, 1, oc).wait_recv()

    lane = lax.broadcasted_iota(jnp.int32, (BLOCK, dim), 1)
    low_lanes = lane < half

    def tiles(block):
        left = jnp.concatenate([kv[block, 0, 0], kv[block, 1, 0]], axis=0).astype(F32)
        right = jnp.concatenate([kv[block, 0, 1], kv[block, 1, 1]], axis=0).astype(F32)
        keys = jnp.where(low_lanes, left, pltpu.roll(right, half, 1))
        values = jnp.where(low_lanes, pltpu.roll(left, half, 1), right)
        return keys, values

    def first_pass(slot, keys, values, usable):
        key_low, value_low = keys.astype(BF16), values.astype(BF16)
        for h in range(heads):
            s = dot(key_low, q4[h], (1, 1))
            if slot == 0:
                place = lax.broadcasted_iota(jnp.int32, (BLOCK, rows), 0)
                query = lax.broadcasted_iota(jnp.int32, (BLOCK, rows), 1) + c * rows
                s = jnp.where(place <= query, s, NEGATIVE)
            m = jnp.max(s, axis=0, keepdims=True)
            e = jnp.exp2((s - m) * rate)
            dp = dot(value_low, g4[h], (1, 1))
            ev[slot, h] = e
            dpv[slot, h] = dp
            top[slot, h] = m if slot == 0 else jnp.where(usable, m, NEGATIVE)
            total[slot, h] = jnp.sum(e, axis=0, keepdims=True)
            prod[slot, h] = jnp.sum(e * dp, axis=0, keepdims=True)
        at = pl.ds(slot * BLOCK, BLOCK)
        k_t[:, at] = keys.T.astype(BF16)
        v_t[:, at] = values.T.astype(BF16)

    forward_x(0)
    if num_blocks > 1:
        forward_z(1)
    for load in loads:
        load.wait()
    settle(0)
    first_pass(0, *tiles(b), None)
    for d in range(2, num_blocks):
        forward_z(d)
        forward_x(d - 1)
    if num_blocks > 1:
        forward_x(num_blocks - 1)
    for d in range(1, num_blocks):
        settle(d)

    offsets = [None] + [picks[b, group, j] for j in range(chosen - 1)]
    for slot in range(1, chosen):
        wanted = b - offsets[slot]
        first_pass(slot, *tiles(jnp.maximum(wanted, 0)), wanted >= 0)

    shares, deltas = [], []
    for h in range(heads):
        m = top[0, h]
        for slot in range(1, chosen):
            m = jnp.maximum(m, top[slot, h])
        weight = [jnp.exp2((top[slot, h] - m) * rate) for slot in range(chosen)]
        norm = sum(weight[slot] * total[slot, h] for slot in range(chosen))
        share = [w / norm for w in weight]
        shares.append(share)
        deltas.append(sum(share[slot] * prod[slot, h] for slot in range(chosen)))

    def core_return(slot):
        return remote(part.at[slot, oc], core_in.at[slot], cs2.at[slot], cr2.at[slot], core_dev)

    def x_return(slot):
        return remote(x_out.at[slot], x_in.at[slot], xs2.at[slot], xr2.at[slot], x_dev)

    def second_pass(slot):
        at = pl.ds(slot * BLOCK, BLOCK)
        grad_k = grad_v = None
        for h in range(heads):
            probs = ev[slot, h] * shares[h][slot]
            low = probs.astype(BF16)
            ds = (probs * (dpv[slot, h] - deltas[h])).astype(BF16)
            p_low[h, at] = low
            ds_low[h, at] = ds
            more_v = dot(low, g4[h], (1, 0))
            more_k = dot(ds, q4[h], (1, 0))
            grad_v = more_v if grad_v is None else grad_v + more_v
            grad_k = more_k if grad_k is None else grad_k + more_k
        grad_k = grad_k * scaling
        left = jnp.where(low_lanes, grad_k, pltpu.roll(grad_v, half, 1)).astype(BF16)
        right = jnp.where(low_lanes, pltpu.roll(grad_k, half, 1), grad_v).astype(BF16)
        for side in range(2):
            cut = slice(side * rows, (side + 1) * rows)
            part[slot, side, 0] = left[cut]
            part[slot, side, 1] = right[cut]
        core_return(slot).start()

    def cross(slot):
        core_return(slot).wait_recv()
        x_out[slot] = (part[slot, c, ox].astype(F32) + core_in[slot, ox].astype(F32)).astype(BF16)
        x_return(slot).start()
        summed[slot] = part[slot, c, x].astype(F32) + core_in[slot, x].astype(F32)

    def land(slot):
        x_return(slot).wait_recv()
        summed[slot] = summed[slot] + x_in[slot].astype(F32)

    def z_return(d):
        return remote(z_out.at[d], z_in.at[d], zs2.at[d], zr2.at[d], (2 * (b - d) + c, head))

    second_pass(1)
    for slot in range(2, chosen):
        second_pass(slot)
        cross(slot - 1)
    second_pass(0)
    cross(chosen - 1)
    cross(0)
    for slot in range(1, chosen):
        land(slot)
    for d in reversed(range(1, num_blocks)):
        @pl.when(d <= b)
        def _():
            z_out[d] = sum(
                jnp.where(offsets[slot] == d, summed[slot], 0.0) for slot in range(1, chosen)
            ).astype(BF16)
            z_return(d).start()

    stores = []
    for h in range(heads):
        attn_buf[h] = dot(v_t[...], p_low[h], (1, 0)).T.astype(BF16)
        dq_buf[h] = dot(k_t[...], ds_low[h], (1, 0)).T * scaling
        cols = pl.ds(h * dim, dim)
        stores.append(pltpu.make_async_copy(attn_buf.at[h], attn_hbm.at[:, cols], out_sem.at[0, h]))
        stores.append(pltpu.make_async_copy(dq_buf.at[h], dq_hbm.at[:, cols], out_sem.at[1, h]))
        stores[-2].start()
        stores[-1].start()

    land(0)
    for d in range(1, num_blocks):
        @pl.when(b + d < num_blocks)
        def _():
            z_return(d).wait_recv()
            summed[0] = summed[0] + z_in[d].astype(F32)
    owned = summed[0]
    dk_out[...] = owned[:, :half]
    dv_out[...] = owned[:, half:]

    for store in stores:
        store.wait()
    for d in range(num_blocks):
        @pl.when(d <= b)
        def _():
            x_gather(d, x).wait_send()
            core_gather(d, 0, c).wait_send()
            core_gather(d, 1, c).wait_send()
    for d in range(1, num_blocks):
        @pl.when(b + d < num_blocks)
        def _():
            z_gather(d).wait_send()
        @pl.when(d <= b)
        def _():
            z_return(d).wait_send()
    for slot in range(chosen):
        core_return(slot).wait_send()
        x_return(slot).wait_send()


def local(queries, key_states, value_states, block_picks, grad_output):
    rows, half = key_states.shape
    dim = 2 * half
    heads = queries.shape[1] // dim
    seq_size = lax.axis_size("seq")
    num_blocks = seq_size * rows // BLOCK
    assert BLOCK == 2 * rows
    chosen = block_picks.shape[2] + 1
    keys = chosen * BLOCK
    vmem = pl.BlockSpec(memory_space=pltpu.VMEM)
    anywhere = pl.BlockSpec(memory_space=pl.ANY)
    dma = pltpu.SemaphoreType.DMA
    return pl.pallas_call(
        functools.partial(kernel, seq_size, chosen),
        out_shape=(
            jax.ShapeDtypeStruct(queries.shape, BF16),
            jax.ShapeDtypeStruct(queries.shape, F32),
            jax.ShapeDtypeStruct(key_states.shape, F32),
            jax.ShapeDtypeStruct(value_states.shape, F32),
        ),
        in_specs=[pl.BlockSpec(memory_space=pltpu.SMEM), vmem, vmem, anywhere, anywhere],
        out_specs=(anywhere, anywhere, vmem, vmem),
        scratch_shapes=[
            pltpu.VMEM((num_blocks, 2, 2, rows, dim), BF16),
            pltpu.VMEM((heads, rows, dim), BF16),
            pltpu.VMEM((heads, rows, dim), BF16),
            pltpu.VMEM((chosen, heads, BLOCK, rows), F32),
            pltpu.VMEM((chosen, heads, BLOCK, rows), F32),
            pltpu.VMEM((heads, keys, rows), BF16),
            pltpu.VMEM((heads, keys, rows), BF16),
            pltpu.VMEM((dim, keys), BF16),
            pltpu.VMEM((dim, keys), BF16),
            pltpu.VMEM((chosen, heads, 1, rows), F32),
            pltpu.VMEM((chosen, heads, 1, rows), F32),
            pltpu.VMEM((chosen, heads, 1, rows), F32),
            pltpu.VMEM((heads, rows, dim), BF16),
            pltpu.VMEM((heads, rows, dim), F32),
            pltpu.VMEM((chosen, 2, 2, rows, dim), BF16),
            pltpu.VMEM((chosen, 2, rows, dim), BF16),
            pltpu.VMEM((chosen, rows, dim), BF16),
            pltpu.VMEM((chosen, rows, dim), BF16),
            pltpu.VMEM((chosen, rows, dim), F32),
            pltpu.VMEM((num_blocks, rows, dim), BF16),
            pltpu.VMEM((num_blocks, rows, dim), BF16),
            dma((2, heads)),
            dma((2, heads)),
            dma((num_blocks,)),
            dma((num_blocks,)),
            dma((num_blocks,)),
            dma((num_blocks,)),
            dma((num_blocks, 2)),
            dma((num_blocks, 2)),
            dma((chosen,)),
            dma((chosen,)),
            dma((chosen,)),
            dma((chosen,)),
            dma((num_blocks,)),
            dma((num_blocks,)),
        ],
        compiler_params=pltpu.CompilerParams(
            collective_id=0, has_side_effects=True, vmem_limit_bytes=56 * 1024 * 1024
        ),
        cost_estimate=pl.CostEstimate(
            flops=10 * heads * rows * keys * dim, bytes_accessed=4 * queries.size * 4, transcendentals=heads * rows * keys
        ),
    )(block_picks, key_states, value_states, queries, grad_output)


def solution(mesh):
    return jax.shard_map(
        local,
        mesh=mesh,
        in_specs=(P("seq", "head"), P("seq", "head"), P("seq", "head"), P(), P("seq", "head")),
        out_specs=(P("seq", "head"), P("seq", "head"), P("seq", "head"), P("seq", "head")),
        check_vma=False,
    )
```

```python
import functools

import jax
import jax.numpy as jnp
from jax import lax
from jax.experimental import pallas as pl
from jax.experimental.pallas import tpu as pltpu
from jax.sharding import PartitionSpec as P

BLOCK = 512
NEGATIVE = -1e30
LOG2E = 1.4426950408889634
MESH = pl.DeviceIdType.MESH
F32 = jnp.float32
BF16 = jnp.bfloat16


def dot(a, b, contract):
    return lax.dot_general(a, b, ((contract[:1], contract[1:]), ((), ())), preferred_element_type=F32)


def kernel(
    seq_size, chosen, picks, k_in, v_in, q_hbm, g_hbm, attn_hbm, dq_hbm, grads_out,
    kv, q4, g4, ev, dpv, p_low, ds_low, k_t, v_t, top, total, prod, attn_buf, dq_buf,
    part, core_in, x_out, x_in, summed, z_out, z_in,
    in_sem, out_sem, zs, zr, xs, xr, cs, cr, cs2, cr2, xs2, xr2, zs2, zr2,
):
    half, rows = k_in.shape
    dim = 2 * half
    heads = q4.shape[0]
    num_blocks = kv.shape[0]
    seq = lax.axis_index("seq")
    head = lax.axis_index("head")
    b, c = seq // 2, seq % 2
    x, group = head % 2, head // 2
    oc, ox = 1 - c, 1 - x
    core_dev = (2 * b + oc, head)
    x_dev = (seq, 2 * group + ox)
    scaling = dim ** (-0.5)
    rate = scaling * LOG2E

    def remote(src, dst, send, recv, dev):
        return pltpu.make_async_remote_copy(
            src_ref=src, dst_ref=dst, send_sem=send, recv_sem=recv, device_id=dev, device_id_type=MESH
        )

    loads = []
    for h in range(heads):
        cols = pl.ds(h * dim, dim)
        loads.append(pltpu.make_async_copy(q_hbm.at[:, cols], q4.at[h], in_sem.at[0, h]))
        loads.append(pltpu.make_async_copy(g_hbm.at[:, cols], g4.at[h], in_sem.at[1, h]))
    for load in loads:
        load.start()

    barrier = pltpu.get_barrier_semaphore()
    pl.semaphore_signal(barrier, inc=1, device_id=core_dev, device_id_type=MESH)
    pl.semaphore_signal(barrier, inc=1, device_id=x_dev, device_id_type=MESH)
    for d in range(1, num_blocks):
        other = lax.rem(b + d, num_blocks)
        pl.semaphore_signal(barrier, inc=1, device_id=(2 * other + c, head), device_id_type=MESH)
    kv[b, c, x, :half] = k_in[...]
    kv[b, c, x, half:] = v_in[...]
    pl.semaphore_wait(barrier, num_blocks + 1)

    def z_gather(d):
        piece = kv.at[b - d, c, x]
        return remote(piece, piece, zs.at[d], zr.at[d + 1], (2 * (b + 1) + c, head))

    def z_arrival(d):
        piece = kv.at[b - d, c, x]
        return remote(piece, piece, zs.at[d], zr.at[d], (2 * (b - 1) + c, head))

    def x_gather(d, side):
        piece = kv.at[b - d, c, side]
        return remote(piece, piece, xs.at[d], xr.at[d], x_dev)

    def core_gather(d, which, row_half):
        piece = kv.at[b - d, row_half, x if which == 0 else ox]
        return remote(piece, piece, cs.at[d, which], cr.at[d, which], core_dev)

    x_gather(0, x).start()
    @pl.when(b + 1 < num_blocks)
    def _():
        z_gather(0).start()
    core_gather(0, 0, c).start()

    def forward_z(d):
        @pl.when(d <= b)
        def _():
            z_arrival(d).wait_recv()
            x_gather(d, x).start()
            if d + 1 < num_blocks:
                @pl.when(b + 1 < num_blocks)
                def _():
                    z_gather(d).start()
            core_gather(d, 0, c).start()

    def forward_x(d):
        @pl.when(d <= b)
        def _():
            x_gather(d, ox).wait_recv()
            core_gather(d, 1, c).start()

    def settle(d):
        @pl.when(d <= b)
        def _():
            core_gather(d, 0, oc).wait_recv()
            core_gather(d, 1, oc).wait_recv()

    lane = lax.broadcasted_iota(jnp.int32, (BLOCK, dim), 1)
    low_lanes = lane < half

    def tiles(block):
        wide = [jnp.concatenate([kv[block, 0, side], kv[block, 1, side]], axis=1) for side in range(2)]
        keys = jnp.concatenate([wide[0][:half], wide[1][:half]], axis=0)
        values = jnp.concatenate([wide[0][half:], wide[1][half:]], axis=0)
        return keys, values

    def first_pass(slot, tiles, usable, which):
        key_low, value_low = (tile.astype(F32).T.astype(BF16) for tile in tiles)
        at = pl.ds(slot * BLOCK, BLOCK)
        k_t[:, at], v_t[:, at] = tiles
        for h in which:
            s = dot(key_low, q4[h], (1, 1))
            if slot == 0:
                place = lax.broadcasted_iota(jnp.int32, (BLOCK, rows), 0)
                query = lax.broadcasted_iota(jnp.int32, (BLOCK, rows), 1) + c * rows
                s = jnp.where(place <= query, s, NEGATIVE)
            m = jnp.max(s, axis=0, keepdims=True)
            e = jnp.exp2((s - m) * rate)
            dp = dot(value_low, g4[h], (1, 1))
            ev[slot, h] = e
            dpv[slot, h] = dp
            top[slot, h] = m if slot == 0 else jnp.where(usable, m, NEGATIVE)
            total[slot, h] = jnp.sum(e, axis=0, keepdims=True)
            prod[slot, h] = jnp.sum(e * dp, axis=0, keepdims=True)

    every = list(range(heads))
    early, late = every[: heads // 2], every[heads // 2 :]
    forward_x(0)
    for d in range(1, min(3, num_blocks)):
        forward_z(d)
        if d == 1:
            forward_x(d)
    for load in loads:
        load.wait()
    settle(0)
    own_tiles = tiles(b)
    first_pass(0, own_tiles, None, early)
    if num_blocks > 2:
        forward_x(2)
    if num_blocks > 3:
        forward_z(3)
    first_pass(0, own_tiles, None, late)
    if num_blocks > 3:
        forward_x(3)
    for d in range(4, num_blocks):
        forward_z(d)
        forward_x(d)
    for d in range(1, num_blocks):
        settle(d)

    offsets = [None] + [picks[group, j, b] for j in range(chosen - 1)]
    for slot in range(1, chosen):
        wanted = b - offsets[slot]
        first_pass(slot, tiles(jnp.maximum(wanted, 0)), wanted >= 0, every)

    shares, deltas = [], []
    for h in range(heads):
        m = top[0, h]
        for slot in range(1, chosen):
            m = jnp.maximum(m, top[slot, h])
        weight = [jnp.exp2((top[slot, h] - m) * rate) for slot in range(chosen)]
        norm = sum(weight[slot] * total[slot, h] for slot in range(chosen))
        share = [w / norm for w in weight]
        shares.append(share)
        deltas.append(sum(share[slot] * prod[slot, h] for slot in range(chosen)))

    def core_return(slot):
        return remote(part.at[slot, oc], core_in.at[slot], cs2.at[slot], cr2.at[slot], core_dev)

    def x_return(slot):
        return remote(x_out.at[slot], x_in.at[slot], xs2.at[slot], xr2.at[slot], x_dev)

    def second_pass(slot, which, before=None):
        at = pl.ds(slot * BLOCK, BLOCK)
        grad_k, grad_v = before or (None, None)
        for h in which:
            probs = ev[slot, h] * shares[h][slot]
            low = probs.astype(BF16)
            ds = (probs * (dpv[slot, h] - deltas[h])).astype(BF16)
            p_low[h, at] = low
            ds_low[h, at] = ds
            more_v = dot(low, g4[h], (1, 0))
            more_k = dot(ds, q4[h], (1, 0))
            grad_v = more_v if grad_v is None else grad_v + more_v
            grad_k = more_k if grad_k is None else grad_k + more_k
        return grad_k, grad_v

    def hand_over(slot, grads):
        grad_k, grad_v = grads
        grad_k = grad_k * scaling
        left = jnp.where(low_lanes, grad_k, pltpu.roll(grad_v, half, 1)).astype(BF16)
        right = jnp.where(low_lanes, pltpu.roll(grad_k, half, 1), grad_v).astype(BF16)
        for side in range(2):
            cut = slice(side * rows, (side + 1) * rows)
            part[slot, side, 0] = left[cut]
            part[slot, side, 1] = right[cut]
        core_return(slot).start()

    def cross(slot):
        core_return(slot).wait_recv()
        x_out[slot] = (part[slot, c, ox].astype(F32) + core_in[slot, ox].astype(F32)).astype(BF16)
        x_return(slot).start()
        summed[slot] = part[slot, c, x].astype(F32) + core_in[slot, x].astype(F32)

    def land(slot):
        x_return(slot).wait_recv()
        summed[slot] = summed[slot] + x_in[slot].astype(F32)

    def z_return(d):
        return remote(z_out.at[d], z_in.at[d], zs2.at[d], zr2.at[d], (2 * (b - d) + c, head))

    for slot in range(1, chosen):
        hand_over(slot, second_pass(slot, every))
        if slot > 1:
            cross(slot - 1)
    grads = second_pass(0, early)
    cross(chosen - 1)
    hand_over(0, second_pass(0, late, grads))
    for slot in range(1, chosen):
        land(slot)
    for d in reversed(range(1, num_blocks)):
        @pl.when(d <= b)
        def _():
            z_out[d] = sum(
                jnp.where(offsets[slot] == d, summed[slot], 0.0) for slot in range(1, chosen)
            ).astype(BF16)
            z_return(d).start()
    cross(0)

    stores = []
    for h in range(heads):
        attn_buf[h] = dot(v_t[...], p_low[h], (1, 0)).T.astype(BF16)
        dq_buf[h] = dot(k_t[...], ds_low[h], (1, 0)).T * scaling
        cols = pl.ds(h * dim, dim)
        stores.append(pltpu.make_async_copy(attn_buf.at[h], attn_hbm.at[:, cols], out_sem.at[0, h]))
        stores.append(pltpu.make_async_copy(dq_buf.at[h], dq_hbm.at[:, cols], out_sem.at[1, h]))
        stores[-2].start()
        stores[-1].start()

    land(0)
    for d in range(1, num_blocks):
        @pl.when(b + d < num_blocks)
        def _():
            z_return(d).wait_recv()
            summed[0] = summed[0] + z_in[d].astype(F32)
    grads_out[...] = summed[0].T

    for store in stores:
        store.wait()
    for d in range(num_blocks):
        @pl.when(d <= b)
        def _():
            x_gather(d, x).wait_send()
            core_gather(d, 0, c).wait_send()
            core_gather(d, 1, c).wait_send()
    for d in range(num_blocks - 1):
        @pl.when((d <= b) & (b + 1 < num_blocks))
        def _():
            z_gather(d).wait_send()
    for d in range(1, num_blocks):
        @pl.when(d <= b)
        def _():
            z_return(d).wait_send()
    for slot in range(chosen):
        core_return(slot).wait_send()
        x_return(slot).wait_send()


def settle_outputs(attn, dq, grads, attn_out, dq_out, dk_out, dv_out, sem):
    rows, half = attn.shape[0], dk_out.shape[0]
    moves = [(grads.at[pl.ds(0, half)], dk_out), (grads.at[pl.ds(half, half)], dv_out)]
    cut = rows // 4
    for i in range(4):
        at = pl.ds(i * cut, cut)
        moves += [(attn.at[at], attn_out.at[at]), (dq.at[at], dq_out.at[at])]
    copies = [pltpu.make_async_copy(src, dst, sem.at[i]) for i, (src, dst) in enumerate(moves)]
    for copy in copies:
        copy.start()
    for copy in copies:
        copy.wait()


def local(queries, key_states, value_states, block_picks, grad_output):
    rows, half = key_states.shape
    dim = 2 * half
    heads = queries.shape[1] // dim
    seq_size = lax.axis_size("seq")
    num_blocks = seq_size * rows // BLOCK
    assert BLOCK == 2 * rows
    chosen = block_picks.shape[2] + 1
    keys = chosen * BLOCK
    vmem = pl.BlockSpec(memory_space=pltpu.VMEM)
    anywhere = pl.BlockSpec(memory_space=pl.ANY)
    dma = pltpu.SemaphoreType.DMA
    attn, dq, grads = pl.pallas_call(
        functools.partial(kernel, seq_size, chosen),
        out_shape=(
            jax.ShapeDtypeStruct(queries.shape, BF16),
            jax.ShapeDtypeStruct(queries.shape, F32),
            jax.ShapeDtypeStruct((dim, rows), F32),
        ),
        in_specs=[pl.BlockSpec(memory_space=pltpu.SMEM), vmem, vmem, anywhere, anywhere],
        out_specs=(anywhere, anywhere, vmem),
        scratch_shapes=[
            pltpu.VMEM((num_blocks, 2, 2, dim, rows), BF16),
            pltpu.VMEM((heads, rows, dim), BF16),
            pltpu.VMEM((heads, rows, dim), BF16),
            pltpu.VMEM((chosen, heads, BLOCK, rows), F32),
            pltpu.VMEM((chosen, heads, BLOCK, rows), F32),
            pltpu.VMEM((heads, keys, rows), BF16),
            pltpu.VMEM((heads, keys, rows), BF16),
            pltpu.VMEM((dim, keys), BF16),
            pltpu.VMEM((dim, keys), BF16),
            pltpu.VMEM((chosen, heads, 1, rows), F32),
            pltpu.VMEM((chosen, heads, 1, rows), F32),
            pltpu.VMEM((chosen, heads, 1, rows), F32),
            pltpu.VMEM((heads, rows, dim), BF16),
            pltpu.VMEM((heads, rows, dim), F32),
            pltpu.VMEM((chosen, 2, 2, rows, dim), BF16),
            pltpu.VMEM((chosen, 2, rows, dim), BF16),
            pltpu.VMEM((chosen, rows, dim), BF16),
            pltpu.VMEM((chosen, rows, dim), BF16),
            pltpu.VMEM((chosen, rows, dim), F32),
            pltpu.VMEM((num_blocks, rows, dim), BF16),
            pltpu.VMEM((num_blocks, rows, dim), BF16),
            dma((2, heads)),
            dma((2, heads)),
            dma((num_blocks,)),
            dma((num_blocks,)),
            dma((num_blocks,)),
            dma((num_blocks,)),
            dma((num_blocks, 2)),
            dma((num_blocks, 2)),
            dma((chosen,)),
            dma((chosen,)),
            dma((chosen,)),
            dma((chosen,)),
            dma((num_blocks,)),
            dma((num_blocks,)),
        ],
        compiler_params=pltpu.CompilerParams(
            collective_id=0, has_side_effects=True, vmem_limit_bytes=56 * 1024 * 1024
        ),
        cost_estimate=pl.CostEstimate(
            flops=10 * heads * rows * keys * dim, bytes_accessed=4 * queries.size * 4, transcendentals=heads * rows * keys
        ),
    )(block_picks.transpose(1, 2, 0), key_states.T, value_states.T, queries, grad_output)
    attn, dq, dk, dv = pl.pallas_call(
        settle_outputs,
        out_shape=(
            jax.ShapeDtypeStruct(attn.shape, attn.dtype),
            jax.ShapeDtypeStruct(dq.shape, dq.dtype),
            jax.ShapeDtypeStruct((half, rows), F32),
            jax.ShapeDtypeStruct((half, rows), F32),
        ),
        in_specs=[anywhere] * 3,
        out_specs=(anywhere,) * 4,
        scratch_shapes=[dma((10,))],
        cost_estimate=pl.CostEstimate(flops=0, bytes_accessed=2 * 7 * queries.size, transcendentals=0),
    )(attn, dq, grads)
    return attn, dq, dk.T, dv.T


def solution(mesh):
    return jax.shard_map(
        local,
        mesh=mesh,
        in_specs=(P("seq", "head"), P("seq", "head"), P("seq", "head"), P(), P("seq", "head")),
        out_specs=(P("seq", "head"), P("seq", "head"), P("seq", "head"), P("seq", "head")),
        check_vma=False,
    )
```

```python
import functools

import jax
import jax.numpy as jnp
from jax import lax
from jax.experimental import pallas as pl
from jax.experimental.pallas import tpu as pltpu
from jax.sharding import PartitionSpec as P

BLOCK = 512
NEGATIVE = -1e30
LOG2E = 1.4426950408889634
MESH = pl.DeviceIdType.MESH
F32 = jnp.float32
BF16 = jnp.bfloat16


def dot(a, b, contract):
    return lax.dot_general(a, b, ((contract[:1], contract[1:]), ((), ())), preferred_element_type=F32)


def kernel(
    seq_size, chosen, picks, k_in, v_in, q_hbm, g_hbm, attn_hbm, dq_hbm, grads_out,
    kv, q4, g4, k_low, v_low, ev, dpv, p_low, ds_low, k_t, v_t, top, total, prod, attn_buf, dq_buf,
    part, core_in, x_out, x_in, summed, z_out, z_in,
    in_sem, out_sem, zs, zr, xs, xr, cs, cr, cs2, cr2, xs2, xr2, zs2, zr2,
):
    half, rows = k_in.shape
    dim = 2 * half
    heads = q4.shape[0]
    num_blocks = kv.shape[0]
    seq = lax.axis_index("seq")
    head = lax.axis_index("head")
    b, c = seq // 2, seq % 2
    x, group = head % 2, head // 2
    oc, ox = 1 - c, 1 - x
    core_dev = (2 * b + oc, head)
    x_dev = (seq, 2 * group + ox)
    scaling = dim ** (-0.5)
    rate = scaling * LOG2E

    def remote(src, dst, send, recv, dev):
        return pltpu.make_async_remote_copy(
            src_ref=src, dst_ref=dst, send_sem=send, recv_sem=recv, device_id=dev, device_id_type=MESH
        )

    loads = []
    for h in range(heads):
        cols = pl.ds(h * dim, dim)
        loads.append(pltpu.make_async_copy(q_hbm.at[:, cols], q4.at[h], in_sem.at[0, h]))
        loads.append(pltpu.make_async_copy(g_hbm.at[:, cols], g4.at[h], in_sem.at[1, h]))
    for load in loads:
        load.start()

    barrier = pltpu.get_barrier_semaphore()
    pl.semaphore_signal(barrier, inc=1, device_id=core_dev, device_id_type=MESH)
    pl.semaphore_signal(barrier, inc=1, device_id=x_dev, device_id_type=MESH)
    for d in range(1, num_blocks):
        other = lax.rem(b + d, num_blocks)
        pl.semaphore_signal(barrier, inc=1, device_id=(2 * other + c, head), device_id_type=MESH)
    kv[b, c, x, :half] = k_in[...]
    kv[b, c, x, half:] = v_in[...]
    pl.semaphore_wait(barrier, num_blocks + 1)

    def z_gather(d):
        piece = kv.at[b - d, c, x]
        return remote(piece, piece, zs.at[d], zr.at[d + 1], (2 * (b + 1) + c, head))

    def z_arrival(d):
        piece = kv.at[b - d, c, x]
        return remote(piece, piece, zs.at[d], zr.at[d], (2 * (b - 1) + c, head))

    def x_gather(d, side):
        piece = kv.at[b - d, c, side]
        return remote(piece, piece, xs.at[d], xr.at[d], x_dev)

    def core_gather(d, which, row_half):
        piece = kv.at[b - d, row_half, x if which == 0 else ox]
        return remote(piece, piece, cs.at[d, which], cr.at[d, which], core_dev)

    x_gather(0, x).start()
    @pl.when(b + 1 < num_blocks)
    def _():
        z_gather(0).start()
    core_gather(0, 0, c).start()

    def forward_z(d):
        @pl.when(d <= b)
        def _():
            z_arrival(d).wait_recv()
            x_gather(d, x).start()
            if d + 1 < num_blocks:
                @pl.when(b + 1 < num_blocks)
                def _():
                    z_gather(d).start()
            core_gather(d, 0, c).start()

    def forward_x(d):
        @pl.when(d <= b)
        def _():
            x_gather(d, ox).wait_recv()
            core_gather(d, 1, c).start()

    def settle(d):
        @pl.when(d <= b)
        def _():
            core_gather(d, 0, oc).wait_recv()
            core_gather(d, 1, oc).wait_recv()

    lane = lax.broadcasted_iota(jnp.int32, (BLOCK, dim), 1)
    low_lanes = lane < half

    def tiles(block):
        wide = [jnp.concatenate([kv[block, 0, side], kv[block, 1, side]], axis=1) for side in range(2)]
        keys = jnp.concatenate([wide[0][:half], wide[1][:half]], axis=0)
        values = jnp.concatenate([wide[0][half:], wide[1][half:]], axis=0)
        return keys, values

    def prepare(slot, block):
        key_tile, value_tile = tiles(block)
        at = pl.ds(pl.multiple_of(slot * BLOCK, BLOCK), BLOCK)
        k_t[:, at] = key_tile
        v_t[:, at] = value_tile
        k_low[slot] = key_tile.astype(F32).T.astype(BF16)
        v_low[slot] = value_tile.astype(F32).T.astype(BF16)

    def first_pass(slot, h, usable, causal):
        s = dot(k_low[slot], q4[h], (1, 1))
        if causal:
            place = lax.broadcasted_iota(jnp.int32, (BLOCK, rows), 0)
            query = lax.broadcasted_iota(jnp.int32, (BLOCK, rows), 1) + c * rows
            s = jnp.where(place <= query, s, NEGATIVE)
        dp = dot(v_low[slot], g4[h], (1, 1))
        m = jnp.max(s, axis=0, keepdims=True)
        e = jnp.exp2((s - m) * rate)
        ev[slot, h] = e
        dpv[slot, h] = dp
        top[slot, h] = m if causal else jnp.where(usable, m, NEGATIVE)
        total[slot, h] = jnp.sum(e, axis=0, keepdims=True)
        prod[slot, h] = jnp.sum(e * dp, axis=0, keepdims=True)

    def own_heads(start, stop):
        @pl.loop(start, stop)
        def _(h):
            first_pass(0, h, None, True)

    forward_x(0)
    for d in range(1, min(3, num_blocks)):
        forward_z(d)
        if d == 1:
            forward_x(d)
    for load in loads:
        load.wait()
    settle(0)
    prepare(0, b)
    own_heads(0, heads // 2)
    if num_blocks > 2:
        forward_x(2)
    if num_blocks > 3:
        forward_z(3)
    own_heads(heads // 2, heads)
    if num_blocks > 3:
        forward_x(3)
    for d in range(4, num_blocks):
        forward_z(d)
        forward_x(d)
    for d in range(1, num_blocks):
        settle(d)

    offsets = [None] + [picks[group, j, b] for j in range(chosen - 1)]
    for slot in range(1, chosen):
        wanted = b - offsets[slot]
        prepare(slot, jnp.maximum(wanted, 0))

        @pl.loop(0, heads)
        def _(h):
            first_pass(slot, h, wanted >= 0, False)

    @pl.loop(0, heads)
    def _(h):
        m = top[0, h]
        for slot in range(1, chosen):
            m = jnp.maximum(m, top[slot, h])
        weight = [jnp.exp2((top[slot, h] - m) * rate) for slot in range(chosen)]
        norm = sum(weight[slot] * total[slot, h] for slot in range(chosen))
        share = [w / norm for w in weight]
        for slot in range(chosen):
            top[slot, h] = share[slot]
        total[0, h] = sum(share[slot] * prod[slot, h] for slot in range(chosen))

    def core_return(slot):
        return remote(part.at[slot, oc], core_in.at[slot], cs2.at[slot], cr2.at[slot], core_dev)

    def x_return(slot):
        return remote(x_out.at[slot], x_in.at[slot], xs2.at[slot], xr2.at[slot], x_dev)

    def second_pass(slot):
        at = pl.ds(pl.multiple_of(slot * BLOCK, BLOCK), BLOCK)

        @pl.loop(0, heads)
        def _(h):
            cols = pl.ds(pl.multiple_of(h * rows, rows), rows)
            probs = ev[slot, h] * top[slot, h]
            p_low[at, cols] = probs.astype(BF16)
            ds_low[at, cols] = (probs * (dpv[slot, h] - total[0, h])).astype(BF16)

    def hand_over(slot):
        at = pl.ds(pl.multiple_of(slot * BLOCK, BLOCK), BLOCK)
        grad_v = dot(p_low[at], g4[...].reshape(heads * rows, dim), (1, 0))
        grad_k = dot(ds_low[at], q4[...].reshape(heads * rows, dim), (1, 0)) * scaling
        left = jnp.where(low_lanes, grad_k, pltpu.roll(grad_v, half, 1)).astype(BF16)
        right = jnp.where(low_lanes, pltpu.roll(grad_k, half, 1), grad_v).astype(BF16)
        for side in range(2):
            cut = slice(side * rows, (side + 1) * rows)
            part[slot, side, 0] = left[cut]
            part[slot, side, 1] = right[cut]
        core_return(slot).start()

    def cross(slot):
        core_return(slot).wait_recv()
        x_out[slot] = (part[slot, c, ox].astype(F32) + core_in[slot, ox].astype(F32)).astype(BF16)
        x_return(slot).start()
        summed[slot] = part[slot, c, x].astype(F32) + core_in[slot, x].astype(F32)

    def land(slot):
        x_return(slot).wait_recv()
        summed[slot] = summed[slot] + x_in[slot].astype(F32)

    def z_return(d):
        return remote(z_out.at[d], z_in.at[d], zs2.at[d], zr2.at[d], (2 * (b - d) + c, head))

    @pl.loop(0, chosen)
    def _(step):
        slot = lax.rem(step + 1, chosen)
        second_pass(slot)

        @pl.when(step > 0)
        def _():
            cross(step)

        hand_over(slot)

    for slot in range(1, chosen):
        land(slot)
    for d in reversed(range(1, num_blocks)):
        @pl.when(d <= b)
        def _():
            z_out[d] = sum(
                jnp.where(offsets[slot] == d, summed[slot], 0.0) for slot in range(1, chosen)
            ).astype(BF16)
            z_return(d).start()
    cross(0)

    attn_buf[...] = dot(v_t[...], p_low[...], (1, 0)).T.astype(BF16)
    dq_buf[...] = (dot(k_t[...], ds_low[...], (1, 0)) * scaling).T
    stores = []
    for h in range(heads):
        at, cols = pl.ds(h * rows, rows), pl.ds(h * dim, dim)
        stores.append(pltpu.make_async_copy(attn_buf.at[at], attn_hbm.at[:, cols], out_sem.at[0, h]))
        stores.append(pltpu.make_async_copy(dq_buf.at[at], dq_hbm.at[:, cols], out_sem.at[1, h]))
        stores[-2].start()
        stores[-1].start()

    land(0)
    for d in range(1, num_blocks):
        @pl.when(b + d < num_blocks)
        def _():
            z_return(d).wait_recv()
            summed[0] = summed[0] + z_in[d].astype(F32)
    grads_out[...] = summed[0].T

    for store in stores:
        store.wait()
    for d in range(num_blocks):
        @pl.when(d <= b)
        def _():
            x_gather(d, x).wait_send()
            core_gather(d, 0, c).wait_send()
            core_gather(d, 1, c).wait_send()
    for d in range(num_blocks - 1):
        @pl.when((d <= b) & (b + 1 < num_blocks))
        def _():
            z_gather(d).wait_send()
    for d in range(1, num_blocks):
        @pl.when(d <= b)
        def _():
            z_return(d).wait_send()
    for slot in range(chosen):
        core_return(slot).wait_send()
        x_return(slot).wait_send()


def settle_outputs(attn, dq, grads, attn_out, dq_out, dk_out, dv_out, attn_buf, dq_buf, grads_buf, sem):
    rows, half = attn.shape[0], dk_out.shape[0]
    cut = rows // 2
    moves = []
    for i in range(2):
        at = pl.ds(i * cut, cut)
        moves.append((dq.at[at], dq_buf.at[at], dq_out.at[at]))
        moves.append((attn.at[at], attn_buf.at[at], attn_out.at[at]))
    for i, out in enumerate((dk_out, dv_out)):
        at = pl.ds(i * half, half)
        moves.append((grads.at[at], grads_buf.at[at], out))
    arrive = [pltpu.make_async_copy(src, mid, sem.at[0, i]) for i, (src, mid, _) in enumerate(moves)]
    leave = [pltpu.make_async_copy(mid, dst, sem.at[1, i]) for i, (_, mid, dst) in enumerate(moves)]
    for copy in arrive:
        copy.start()
    for first, then in zip(arrive, leave):
        first.wait()
        then.start()
    for copy in leave:
        copy.wait()


def local(queries, key_states, value_states, block_picks, grad_output):
    rows, half = key_states.shape
    dim = 2 * half
    heads = queries.shape[1] // dim
    seq_size = lax.axis_size("seq")
    num_blocks = seq_size * rows // BLOCK
    assert BLOCK == 2 * rows
    chosen = block_picks.shape[2] + 1
    keys = chosen * BLOCK
    vmem = pl.BlockSpec(memory_space=pltpu.VMEM)
    anywhere = pl.BlockSpec(memory_space=pl.ANY)
    dma = pltpu.SemaphoreType.DMA
    attn, dq, grads = pl.pallas_call(
        functools.partial(kernel, seq_size, chosen),
        out_shape=(
            jax.ShapeDtypeStruct(queries.shape, BF16),
            jax.ShapeDtypeStruct(queries.shape, F32),
            jax.ShapeDtypeStruct((dim, rows), F32),
        ),
        in_specs=[pl.BlockSpec(memory_space=pltpu.SMEM), vmem, vmem, anywhere, anywhere],
        out_specs=(anywhere, anywhere, vmem),
        scratch_shapes=[
            pltpu.VMEM((num_blocks, 2, 2, dim, rows), BF16),
            pltpu.VMEM((heads, rows, dim), BF16),
            pltpu.VMEM((heads, rows, dim), BF16),
            pltpu.VMEM((chosen, BLOCK, dim), BF16),
            pltpu.VMEM((chosen, BLOCK, dim), BF16),
            pltpu.VMEM((chosen, heads, BLOCK, rows), F32),
            pltpu.VMEM((chosen, heads, BLOCK, rows), F32),
            pltpu.VMEM((keys, heads * rows), BF16),
            pltpu.VMEM((keys, heads * rows), BF16),
            pltpu.VMEM((dim, keys), BF16),
            pltpu.VMEM((dim, keys), BF16),
            pltpu.VMEM((chosen, heads, 1, rows), F32),
            pltpu.VMEM((chosen, heads, 1, rows), F32),
            pltpu.VMEM((chosen, heads, 1, rows), F32),
            pltpu.VMEM((heads * rows, dim), BF16),
            pltpu.VMEM((heads * rows, dim), F32),
            pltpu.VMEM((chosen, 2, 2, rows, dim), BF16),
            pltpu.VMEM((chosen, 2, rows, dim), BF16),
            pltpu.VMEM((chosen, rows, dim), BF16),
            pltpu.VMEM((chosen, rows, dim), BF16),
            pltpu.VMEM((chosen, rows, dim), F32),
            pltpu.VMEM((num_blocks, rows, dim), BF16),
            pltpu.VMEM((num_blocks, rows, dim), BF16),
            dma((2, heads)),
            dma((2, heads)),
            dma((num_blocks,)),
            dma((num_blocks,)),
            dma((num_blocks,)),
            dma((num_blocks,)),
            dma((num_blocks, 2)),
            dma((num_blocks, 2)),
            dma((chosen,)),
            dma((chosen,)),
            dma((chosen,)),
            dma((chosen,)),
            dma((num_blocks,)),
            dma((num_blocks,)),
        ],
        compiler_params=pltpu.CompilerParams(
            collective_id=0, has_side_effects=True, vmem_limit_bytes=56 * 1024 * 1024
        ),
        cost_estimate=pl.CostEstimate(
            flops=10 * heads * rows * keys * dim, bytes_accessed=4 * queries.size * 4, transcendentals=heads * rows * keys
        ),
    )(block_picks.transpose(1, 2, 0), key_states.T, value_states.T, queries, grad_output)
    attn, dq, dk, dv = pl.pallas_call(
        settle_outputs,
        out_shape=(
            jax.ShapeDtypeStruct(attn.shape, attn.dtype),
            jax.ShapeDtypeStruct(dq.shape, dq.dtype),
            jax.ShapeDtypeStruct((half, rows), F32),
            jax.ShapeDtypeStruct((half, rows), F32),
        ),
        in_specs=[anywhere] * 3,
        out_specs=(anywhere,) * 4,
        scratch_shapes=[
            pltpu.VMEM(attn.shape, attn.dtype),
            pltpu.VMEM(dq.shape, dq.dtype),
            pltpu.VMEM(grads.shape, grads.dtype),
            dma((2, 6)),
        ],
        cost_estimate=pl.CostEstimate(flops=0, bytes_accessed=2 * 7 * queries.size, transcendentals=0),
    )(attn, dq, grads)
    return attn, dq, dk.T, dv.T


def solution(mesh):
    return jax.shard_map(
        local,
        mesh=mesh,
        in_specs=(P("seq", "head"), P("seq", "head"), P("seq", "head"), P(), P("seq", "head")),
        out_specs=(P("seq", "head"), P("seq", "head"), P("seq", "head"), P("seq", "head")),
        check_vma=False,
    )
```

```python
import functools

import jax
import jax.numpy as jnp
from jax import lax
from jax.experimental import pallas as pl
from jax.experimental.pallas import tpu as pltpu
from jax.sharding import PartitionSpec as P

BLOCK = 512
NEGATIVE = -1e30
LOG2E = 1.4426950408889634
MESH = pl.DeviceIdType.MESH
F32 = jnp.float32
BF16 = jnp.bfloat16


def dot(a, b, contract):
    return lax.dot_general(a, b, ((contract[:1], contract[1:]), ((), ())), preferred_element_type=F32)


def kernel(
    seq_size, chosen, picks, k_in, v_in, q_hbm, g_hbm, attn_hbm, dq_hbm, grads_out,
    kv, q4, g4, k_low, v_low, ev, dpv, p_low, ds_low, k_t, v_t, top, total, prod, attn_buf, dq_buf,
    part, core_in, x_out, x_in, summed, z_out, z_in,
    in_sem, out_sem, zs, zr, xs, xr, cs, cr, cs2, cr2, xs2, xr2, zs2, zr2,
):
    half, rows = k_in.shape
    dim = 2 * half
    heads = q4.shape[0]
    num_blocks = kv.shape[0]
    seq = lax.axis_index("seq")
    head = lax.axis_index("head")
    b, c = seq // 2, seq % 2
    x, group = head % 2, head // 2
    oc, ox = 1 - c, 1 - x
    core_dev = (2 * b + oc, head)
    x_dev = (seq, 2 * group + ox)
    scaling = dim ** (-0.5)
    rate = scaling * LOG2E
    part_rows = rows // 2

    def remote(src, dst, send, recv, dev):
        return pltpu.make_async_remote_copy(
            src_ref=src, dst_ref=dst, send_sem=send, recv_sem=recv, device_id=dev, device_id_type=MESH
        )

    loads = []
    for h in range(heads):
        cols = pl.ds(h * dim, dim)
        loads.append(pltpu.make_async_copy(q_hbm.at[:, cols], q4.at[h], in_sem.at[0, h]))
        loads.append(pltpu.make_async_copy(g_hbm.at[:, cols], g4.at[h], in_sem.at[1, h]))
    for load in loads:
        load.start()

    barrier = pltpu.get_barrier_semaphore()
    pl.semaphore_signal(barrier, inc=1, device_id=core_dev, device_id_type=MESH)
    pl.semaphore_signal(barrier, inc=1, device_id=x_dev, device_id_type=MESH)
    for d in range(1, num_blocks):
        other = lax.rem(b + d, num_blocks)
        pl.semaphore_signal(barrier, inc=1, device_id=(2 * other + c, head), device_id_type=MESH)
    kv[b, c, x, :half] = k_in[...]
    kv[b, c, x, half:] = v_in[...]
    pl.semaphore_wait(barrier, num_blocks + 1)

    def z_gather(d):
        piece = kv.at[b - d, c, x]
        return remote(piece, piece, zs.at[d], zr.at[d + 1], (2 * (b + 1) + c, head))

    def z_arrival(d):
        piece = kv.at[b - d, c, x]
        return remote(piece, piece, zs.at[d], zr.at[d], (2 * (b - 1) + c, head))

    def x_gather(d, side):
        piece = kv.at[b - d, c, side]
        return remote(piece, piece, xs.at[d], xr.at[d], x_dev)

    def core_gather(d, which, row_half):
        piece = kv.at[b - d, row_half, x if which == 0 else ox]
        return remote(piece, piece, cs.at[d, which], cr.at[d, which], core_dev)

    x_gather(0, x).start()
    @pl.when(b + 1 < num_blocks)
    def _():
        z_gather(0).start()
    core_gather(0, 0, c).start()

    def forward_z(d):
        @pl.when(d <= b)
        def _():
            z_arrival(d).wait_recv()
            x_gather(d, x).start()
            if d + 1 < num_blocks:
                @pl.when(b + 1 < num_blocks)
                def _():
                    z_gather(d).start()
            core_gather(d, 0, c).start()

    def forward_x(d):
        @pl.when(d <= b)
        def _():
            x_gather(d, ox).wait_recv()
            core_gather(d, 1, c).start()

    def settle(d):
        @pl.when(d <= b)
        def _():
            core_gather(d, 0, oc).wait_recv()
            core_gather(d, 1, oc).wait_recv()

    def tiles(block):
        wide = [jnp.concatenate([kv[block, 0, side], kv[block, 1, side]], axis=1) for side in range(2)]
        keys = jnp.concatenate([wide[0][:half], wide[1][:half]], axis=0)
        values = jnp.concatenate([wide[0][half:], wide[1][half:]], axis=0)
        return keys, values

    def prepare(slot, block):
        key_tile, value_tile = tiles(block)
        for piece in range(4):
            side, chunk = piece % 2, piece // 2
            cut = slice(side * rows + chunk * part_rows, side * rows + (chunk + 1) * part_rows)
            at = pl.ds(pl.multiple_of(slot * BLOCK + piece * part_rows, part_rows), part_rows)
            k_t[:, at] = key_tile[:, cut]
            v_t[:, at] = value_tile[:, cut]
        k_low[slot] = key_tile.astype(F32).T.astype(BF16)
        v_low[slot] = value_tile.astype(F32).T.astype(BF16)

    def first_pass(slot, which, usable, causal):
        for h in which:
            s = dot(k_low[slot], q4[h], (1, 1))
            if causal:
                place = lax.broadcasted_iota(jnp.int32, (BLOCK, rows), 0)
                query = lax.broadcasted_iota(jnp.int32, (BLOCK, rows), 1) + c * rows
                s = jnp.where(place <= query, s, NEGATIVE)
            dp = dot(v_low[slot], g4[h], (1, 1))
            m = jnp.max(s, axis=0, keepdims=True)
            e = jnp.exp2((s - m) * rate)
            for piece in range(4):
                side, chunk = piece % 2, piece // 2
                cut = slice(side * rows + chunk * part_rows, side * rows + (chunk + 1) * part_rows)
                at = slice(side * part_rows, (side + 1) * part_rows)
                ev[2 * slot + chunk, h, at] = e[cut]
                dpv[2 * slot + chunk, h, at] = dp[cut]
            top[slot, h] = m if causal else jnp.where(usable, m, NEGATIVE)
            total[slot, h] = jnp.sum(e, axis=0, keepdims=True)
            prod[slot, h] = jnp.sum(e * dp, axis=0, keepdims=True)

    every = list(range(heads))
    forward_x(0)
    for d in range(1, min(3, num_blocks)):
        forward_z(d)
        if d == 1:
            forward_x(d)
    for load in loads:
        load.wait()
    settle(0)
    prepare(0, b)
    first_pass(0, every[: heads // 2], None, True)
    if num_blocks > 2:
        forward_x(2)
    if num_blocks > 3:
        forward_z(3)
    first_pass(0, every[heads // 2 :], None, True)
    if num_blocks > 3:
        forward_x(3)
    for d in range(4, num_blocks):
        forward_z(d)
        forward_x(d)
    for d in range(1, num_blocks):
        settle(d)

    offsets = [None] + [picks[group, j, b] for j in range(chosen - 1)]
    @pl.loop(1, chosen)
    def _(slot):
        wanted = b - picks[group, slot - 1, b]
        prepare(slot, jnp.maximum(wanted, 0))
        first_pass(slot, every, wanted >= 0, False)

    for h in every:
        m = top[0, h]
        for slot in range(1, chosen):
            m = jnp.maximum(m, top[slot, h])
        weight = [jnp.exp2((top[slot, h] - m) * rate) for slot in range(chosen)]
        norm = sum(weight[slot] * total[slot, h] for slot in range(chosen))
        share = [w / norm for w in weight]
        for slot in range(chosen):
            top[slot, h] = share[slot]
        total[0, h] = sum(share[slot] * prod[slot, h] for slot in range(chosen))

    def core_return(unit):
        return remote(part.at[unit, oc], core_in.at[unit], cs2.at[unit], cr2.at[unit], core_dev)

    def x_return(unit):
        return remote(x_out.at[unit], x_in.at[unit], xs2.at[unit], xr2.at[unit], x_dev)

    def z_return(d, chunk):
        return remote(
            z_out.at[d, chunk], z_in.at[d, chunk], zs2.at[d, chunk], zr2.at[d, chunk], (2 * (b - d) + c, head)
        )

    def second_pass(unit):
        slot = unit // 2
        at = pl.ds(pl.multiple_of(unit * 2 * part_rows, 2 * part_rows), 2 * part_rows)
        grad_k = grad_v = 0.0
        for h in every:
            cols = slice(h * rows, (h + 1) * rows)
            probs = ev[unit, h] * top[slot, h]
            low = probs.astype(BF16)
            ds = (probs * (dpv[unit, h] - total[0, h])).astype(BF16)
            p_low[at, cols] = low
            ds_low[at, cols] = ds
            grad_v += dot(low, g4[h], (1, 0))
            grad_k += dot(ds, q4[h], (1, 0))
        grad_k = grad_k * scaling
        lanes = lax.broadcasted_iota(jnp.int32, grad_k.shape, 1) < half
        left = jnp.where(lanes, grad_k, pltpu.roll(grad_v, half, 1)).astype(BF16)
        right = jnp.where(lanes, pltpu.roll(grad_k, half, 1), grad_v).astype(BF16)
        for side in range(2):
            cut = slice(side * part_rows, (side + 1) * part_rows)
            part[unit, side, 0] = left[cut]
            part[unit, side, 1] = right[cut]
        core_return(unit).start()

    def cross(unit):
        core_return(unit).wait_recv()
        x_out[unit] = (part[unit, c, ox].astype(F32) + core_in[unit, ox].astype(F32)).astype(BF16)
        x_return(unit).start()
        summed[unit] = part[unit, c, x].astype(F32) + core_in[unit, x].astype(F32)

    def land(unit):
        x_return(unit).wait_recv()
        summed[unit] = summed[unit] + x_in[unit].astype(F32)

    def send_back(chunk):
        for slot in range(1, chosen):
            land(2 * slot + chunk)
        for d in reversed(range(1, num_blocks)):
            @pl.when(d <= b)
            def _():
                z_out[d, chunk] = sum(
                    jnp.where(picks[group, slot - 1, b] == d, summed[2 * slot + chunk], 0.0)
                    for slot in range(1, chosen)
                ).astype(BF16)
                z_return(d, chunk).start()

    others = chosen - 1

    def unit_of(step):
        tail = step // (2 * others)
        slot = (1 - tail) * (1 + step % others)
        return 2 * slot + (1 - tail) * (step // others) + tail * (step - 2 * others)

    @pl.loop(0, 2 * chosen)
    def _(step):
        second_pass(unit_of(step))

        @pl.when(step > 0)
        def _():
            cross(unit_of(step - 1))

        @pl.when(step == 2 * others - 1)
        def _():
            send_back(0)

    send_back(1)
    cross(1)

    attn_buf[...] = dot(v_t[...], p_low[...], (1, 0)).T.astype(BF16)
    dq_buf[...] = (dot(k_t[...], ds_low[...], (1, 0)) * scaling).T
    stores = []
    for h in range(heads):
        at, cols = pl.ds(h * rows, rows), pl.ds(h * dim, dim)
        stores.append(pltpu.make_async_copy(attn_buf.at[at], attn_hbm.at[:, cols], out_sem.at[0, h]))
        stores.append(pltpu.make_async_copy(dq_buf.at[at], dq_hbm.at[:, cols], out_sem.at[1, h]))
        stores[-2].start()
        stores[-1].start()

    for chunk in range(2):
        land(chunk)
        for d in range(1, num_blocks):
            @pl.when(b + d < num_blocks)
            def _():
                z_return(d, chunk).wait_recv()
                summed[chunk] = summed[chunk] + z_in[d, chunk].astype(F32)
        at = pl.ds(chunk * part_rows, part_rows)
        grads_out[:, at] = summed[chunk].T

    for store in stores:
        store.wait()
    for d in range(num_blocks):
        @pl.when(d <= b)
        def _():
            x_gather(d, x).wait_send()
            core_gather(d, 0, c).wait_send()
            core_gather(d, 1, c).wait_send()
    for d in range(num_blocks - 1):
        @pl.when((d <= b) & (b + 1 < num_blocks))
        def _():
            z_gather(d).wait_send()
    for d in range(1, num_blocks):
        @pl.when(d <= b)
        def _():
            z_return(d, 0).wait_send()
            z_return(d, 1).wait_send()
    for unit in range(2 * chosen):
        core_return(unit).wait_send()
        x_return(unit).wait_send()


def settle_outputs(attn, dq, grads, attn_out, dq_out, dk_out, dv_out, attn_buf, dq_buf, grads_buf, sem):
    rows, half = attn.shape[0], dk_out.shape[0]
    cut = rows // 2
    moves = []
    for i in range(2):
        at = pl.ds(i * cut, cut)
        moves.append((dq.at[at], dq_buf.at[at], dq_out.at[at]))
        moves.append((attn.at[at], attn_buf.at[at], attn_out.at[at]))
    for i, out in enumerate((dk_out, dv_out)):
        at = pl.ds(i * half, half)
        moves.append((grads.at[at], grads_buf.at[at], out))
    arrive = [pltpu.make_async_copy(src, mid, sem.at[0, i]) for i, (src, mid, _) in enumerate(moves)]
    leave = [pltpu.make_async_copy(mid, dst, sem.at[1, i]) for i, (_, mid, dst) in enumerate(moves)]
    for copy in arrive:
        copy.start()
    for first, then in zip(arrive, leave):
        first.wait()
        then.start()
    for copy in leave:
        copy.wait()


def local(queries, key_states, value_states, block_picks, grad_output):
    rows, half = key_states.shape
    dim = 2 * half
    heads = queries.shape[1] // dim
    seq_size = lax.axis_size("seq")
    num_blocks = seq_size * rows // BLOCK
    assert BLOCK == 2 * rows
    chosen = block_picks.shape[2] + 1
    keys = chosen * BLOCK
    vmem = pl.BlockSpec(memory_space=pltpu.VMEM)
    anywhere = pl.BlockSpec(memory_space=pl.ANY)
    dma = pltpu.SemaphoreType.DMA
    attn, dq, grads = pl.pallas_call(
        functools.partial(kernel, seq_size, chosen),
        out_shape=(
            jax.ShapeDtypeStruct(queries.shape, BF16),
            jax.ShapeDtypeStruct(queries.shape, F32),
            jax.ShapeDtypeStruct((dim, rows), F32),
        ),
        in_specs=[pl.BlockSpec(memory_space=pltpu.SMEM), vmem, vmem, anywhere, anywhere],
        out_specs=(anywhere, anywhere, vmem),
        scratch_shapes=[
            pltpu.VMEM((num_blocks, 2, 2, dim, rows), BF16),
            pltpu.VMEM((heads, rows, dim), BF16),
            pltpu.VMEM((heads, rows, dim), BF16),
            pltpu.VMEM((chosen, BLOCK, dim), BF16),
            pltpu.VMEM((chosen, BLOCK, dim), BF16),
            pltpu.VMEM((2 * chosen, heads, rows, rows), F32),
            pltpu.VMEM((2 * chosen, heads, rows, rows), F32),
            pltpu.VMEM((keys, heads * rows), BF16),
            pltpu.VMEM((keys, heads * rows), BF16),
            pltpu.VMEM((dim, keys), BF16),
            pltpu.VMEM((dim, keys), BF16),
            pltpu.VMEM((chosen, heads, 1, rows), F32),
            pltpu.VMEM((chosen, heads, 1, rows), F32),
            pltpu.VMEM((chosen, heads, 1, rows), F32),
            pltpu.VMEM((heads * rows, dim), BF16),
            pltpu.VMEM((heads * rows, dim), F32),
            pltpu.VMEM((2 * chosen, 2, 2, rows // 2, dim), BF16),
            pltpu.VMEM((2 * chosen, 2, rows // 2, dim), BF16),
            pltpu.VMEM((2 * chosen, rows // 2, dim), BF16),
            pltpu.VMEM((2 * chosen, rows // 2, dim), BF16),
            pltpu.VMEM((2 * chosen, rows // 2, dim), F32),
            pltpu.VMEM((num_blocks, 2, rows // 2, dim), BF16),
            pltpu.VMEM((num_blocks, 2, rows // 2, dim), BF16),
            dma((2, heads)),
            dma((2, heads)),
            dma((num_blocks,)),
            dma((num_blocks,)),
            dma((num_blocks,)),
            dma((num_blocks,)),
            dma((num_blocks, 2)),
            dma((num_blocks, 2)),
            dma((2 * chosen,)),
            dma((2 * chosen,)),
            dma((2 * chosen,)),
            dma((2 * chosen,)),
            dma((num_blocks, 2)),
            dma((num_blocks, 2)),
        ],
        compiler_params=pltpu.CompilerParams(
            collective_id=0, has_side_effects=True, vmem_limit_bytes=56 * 1024 * 1024
        ),
        cost_estimate=pl.CostEstimate(
            flops=10 * heads * rows * keys * dim, bytes_accessed=4 * queries.size * 4, transcendentals=heads * rows * keys
        ),
    )(block_picks.transpose(1, 2, 0), key_states.T, value_states.T, queries, grad_output)
    attn, dq, dk, dv = pl.pallas_call(
        settle_outputs,
        out_shape=(
            jax.ShapeDtypeStruct(attn.shape, attn.dtype),
            jax.ShapeDtypeStruct(dq.shape, dq.dtype),
            jax.ShapeDtypeStruct((half, rows), F32),
            jax.ShapeDtypeStruct((half, rows), F32),
        ),
        in_specs=[anywhere] * 3,
        out_specs=(anywhere,) * 4,
        scratch_shapes=[
            pltpu.VMEM(attn.shape, attn.dtype),
            pltpu.VMEM(dq.shape, dq.dtype),
            pltpu.VMEM(grads.shape, grads.dtype),
            dma((2, 6)),
        ],
        cost_estimate=pl.CostEstimate(flops=0, bytes_accessed=2 * 7 * queries.size, transcendentals=0),
    )(attn, dq, grads)
    return attn, dq, dk.T, dv.T


def solution(mesh):
    return jax.shard_map(
        local,
        mesh=mesh,
        in_specs=(P("seq", "head"), P("seq", "head"), P("seq", "head"), P(), P("seq", "head")),
        out_specs=(P("seq", "head"), P("seq", "head"), P("seq", "head"), P("seq", "head")),
        check_vma=False,
    )
```

```python
import functools

import jax
import jax.numpy as jnp
from jax import lax
from jax.experimental import pallas as pl
from jax.experimental.pallas import tpu as pltpu
from jax.sharding import PartitionSpec as P

BLOCK = 512
NEGATIVE = -1e30
LOG2E = 1.4426950408889634
MESH = pl.DeviceIdType.MESH
F32 = jnp.float32
BF16 = jnp.bfloat16


def dot(a, b, contract):
    return lax.dot_general(a, b, ((contract[:1], contract[1:]), ((), ())), preferred_element_type=F32)


def places():
    seq = lax.axis_index("seq")
    head = lax.axis_index("head")
    b, c = seq // 2, seq % 2
    x, group = head % 2, head // 2
    return head, group, b, c, 1 - c, x, 1 - x, (2 * b + 1 - c, head), (seq, 2 * group + 1 - x)


def remote(src, dst, send, recv, dev):
    return pltpu.make_async_remote_copy(
        src_ref=src, dst_ref=dst, send_sem=send, recv_sem=recv, device_id=dev, device_id_type=MESH
    )


def greet(devices):
    barrier = pltpu.get_barrier_semaphore()
    for device in devices:
        pl.semaphore_signal(barrier, inc=1, device_id=device, device_id_type=MESH)
    pl.semaphore_wait(barrier, len(devices))


def gather(k_in, v_in, kv, zs, zr, xs, xr, cs, cr):
    half = k_in.shape[0]
    num_blocks = kv.shape[0]
    head, group, b, c, oc, x, ox, core_dev, x_dev = places()
    kv[b, c, x, :half] = k_in[...]
    kv[b, c, x, half:] = v_in[...]
    greet([core_dev, x_dev] + [(2 * lax.rem(b + d, num_blocks) + c, head) for d in range(1, num_blocks)])

    def z_gather(d):
        piece = kv.at[b - d, c, x]
        return remote(piece, piece, zs.at[d], zr.at[d + 1], (2 * (b + 1) + c, head))

    def z_arrival(d):
        piece = kv.at[b - d, c, x]
        return remote(piece, piece, zs.at[d], zr.at[d], (2 * (b - 1) + c, head))

    def x_gather(d, side):
        piece = kv.at[b - d, c, side]
        return remote(piece, piece, xs.at[d], xr.at[d], x_dev)

    def core_gather(d, which, row_half):
        piece = kv.at[b - d, row_half, x if which == 0 else ox]
        return remote(piece, piece, cs.at[d, which], cr.at[d, which], core_dev)

    x_gather(0, x).start()
    @pl.when(b + 1 < num_blocks)
    def _():
        z_gather(0).start()
    core_gather(0, 0, c).start()

    def forward_z(d):
        @pl.when(d <= b)
        def _():
            z_arrival(d).wait_recv()
            x_gather(d, x).start()
            if d + 1 < num_blocks:
                @pl.when(b + 1 < num_blocks)
                def _():
                    z_gather(d).start()
            core_gather(d, 0, c).start()

    def forward_x(d):
        @pl.when(d <= b)
        def _():
            x_gather(d, ox).wait_recv()
            core_gather(d, 1, c).start()

    def settle(d):
        @pl.when(d <= b)
        def _():
            core_gather(d, 0, oc).wait_recv()
            core_gather(d, 1, oc).wait_recv()

    forward_x(0)
    for d in range(1, num_blocks):
        forward_z(d)
        forward_x(d - 1) if d > 1 else None
    if num_blocks > 1:
        forward_x(num_blocks - 1)
    for d in range(num_blocks):
        settle(d)
    for d in range(num_blocks):
        @pl.when(d <= b)
        def _():
            x_gather(d, x).wait_send()
            core_gather(d, 0, c).wait_send()
            core_gather(d, 1, c).wait_send()
    for d in range(num_blocks - 1):
        @pl.when((d <= b) & (b + 1 < num_blocks))
        def _():
            z_gather(d).wait_send()


def compute(
    chosen, picks, kv, q_hbm, g_hbm, attn_hbm, dq_hbm, part,
    q4, g4, k_low, v_low, ev, dpv, p_low, ds_low, k_t, v_t, top, total, prod, attn_buf, dq_buf, in_sem, out_sem,
):
    dim, rows = kv.shape[3:]
    half = dim // 2
    heads = q4.shape[0]
    head, group, b, c = places()[:4]
    scaling = dim ** (-0.5)
    rate = scaling * LOG2E
    part_rows = rows // 2

    loads = []
    for h in range(heads):
        cols = pl.ds(h * dim, dim)
        loads.append(pltpu.make_async_copy(q_hbm.at[:, cols], q4.at[h], in_sem.at[0, h]))
        loads.append(pltpu.make_async_copy(g_hbm.at[:, cols], g4.at[h], in_sem.at[1, h]))
    for load in loads:
        load.start()

    def tiles(block):
        wide = [jnp.concatenate([kv[block, 0, side], kv[block, 1, side]], axis=1) for side in range(2)]
        keys = jnp.concatenate([wide[0][:half], wide[1][:half]], axis=0)
        values = jnp.concatenate([wide[0][half:], wide[1][half:]], axis=0)
        return keys, values

    def prepare(slot, block):
        key_tile, value_tile = tiles(block)
        for piece in range(4):
            side, chunk = piece % 2, piece // 2
            cut = slice(side * rows + chunk * part_rows, side * rows + (chunk + 1) * part_rows)
            at = pl.ds(pl.multiple_of(slot * BLOCK + piece * part_rows, part_rows), part_rows)
            k_t[:, at] = key_tile[:, cut]
            v_t[:, at] = value_tile[:, cut]
        k_low[slot] = key_tile.astype(F32).T.astype(BF16)
        v_low[slot] = value_tile.astype(F32).T.astype(BF16)

    def first_pass(slot, which, usable, causal):
        for h in which:
            s = dot(k_low[slot], q4[h], (1, 1))
            if causal:
                place = lax.broadcasted_iota(jnp.int32, (BLOCK, rows), 0)
                query = lax.broadcasted_iota(jnp.int32, (BLOCK, rows), 1) + c * rows
                s = jnp.where(place <= query, s, NEGATIVE)
            dp = dot(v_low[slot], g4[h], (1, 1))
            m = jnp.max(s, axis=0, keepdims=True)
            e = jnp.exp2((s - m) * rate)
            for piece in range(4):
                side, chunk = piece % 2, piece // 2
                cut = slice(side * rows + chunk * part_rows, side * rows + (chunk + 1) * part_rows)
                at = slice(side * part_rows, (side + 1) * part_rows)
                ev[2 * slot + chunk, h, at] = e[cut]
                dpv[2 * slot + chunk, h, at] = dp[cut]
            top[slot, h] = m if causal else jnp.where(usable, m, NEGATIVE)
            total[slot, h] = jnp.sum(e, axis=0, keepdims=True)
            prod[slot, h] = jnp.sum(e * dp, axis=0, keepdims=True)

    every = list(range(heads))
    prepare(0, b)
    for load in loads:
        load.wait()
    first_pass(0, every, None, True)

    @pl.loop(1, chosen)
    def _(slot):
        wanted = b - picks[group, slot - 1, b]
        prepare(slot, jnp.maximum(wanted, 0))
        first_pass(slot, every, wanted >= 0, False)

    for h in every:
        m = top[0, h]
        for slot in range(1, chosen):
            m = jnp.maximum(m, top[slot, h])
        weight = [jnp.exp2((top[slot, h] - m) * rate) for slot in range(chosen)]
        norm = sum(weight[slot] * total[slot, h] for slot in range(chosen))
        share = [w / norm for w in weight]
        for slot in range(chosen):
            top[slot, h] = share[slot]
        total[0, h] = sum(share[slot] * prod[slot, h] for slot in range(chosen))

    def second_pass(unit):
        slot = unit // 2
        at = pl.ds(pl.multiple_of(unit * 2 * part_rows, 2 * part_rows), 2 * part_rows)
        grad_k = grad_v = 0.0
        for h in every:
            cols = slice(h * rows, (h + 1) * rows)
            probs = ev[unit, h] * top[slot, h]
            low = probs.astype(BF16)
            ds = (probs * (dpv[unit, h] - total[0, h])).astype(BF16)
            p_low[at, cols] = low
            ds_low[at, cols] = ds
            grad_v += dot(low, g4[h], (1, 0))
            grad_k += dot(ds, q4[h], (1, 0))
        grad_k = grad_k * scaling
        lanes = lax.broadcasted_iota(jnp.int32, grad_k.shape, 1) < half
        left = jnp.where(lanes, grad_k, pltpu.roll(grad_v, half, 1)).astype(BF16)
        right = jnp.where(lanes, pltpu.roll(grad_k, half, 1), grad_v).astype(BF16)
        for side in range(2):
            cut = slice(side * part_rows, (side + 1) * part_rows)
            part[unit, side, 0] = left[cut]
            part[unit, side, 1] = right[cut]

    @pl.loop(0, 2 * chosen)
    def _(unit):
        second_pass(unit)

    attn_buf[...] = dot(v_t[...], p_low[...], (1, 0)).T.astype(BF16)
    dq_buf[...] = (dot(k_t[...], ds_low[...], (1, 0)) * scaling).T
    stores = []
    for h in range(heads):
        at, cols = pl.ds(h * rows, rows), pl.ds(h * dim, dim)
        stores.append(pltpu.make_async_copy(attn_buf.at[at], attn_hbm.at[:, cols], out_sem.at[0, h]))
        stores.append(pltpu.make_async_copy(dq_buf.at[at], dq_hbm.at[:, cols], out_sem.at[1, h]))
        stores[-2].start()
        stores[-1].start()

    for store in stores:
        store.wait()


def give_back(chosen, picks, part, grads_out, core_in, x_out, x_in, summed, z_out, z_in, cs2, cr2, xs2, xr2, zs2, zr2):
    num_blocks = z_in.shape[0]
    part_rows = part.shape[3]
    head, group, b, c, oc, x, ox, core_dev, x_dev = places()
    greet([core_dev, x_dev] + [(2 * lax.rem(b + d, num_blocks) + c, head) for d in range(1, num_blocks)])

    def core_return(unit):
        return remote(part.at[unit, oc], core_in.at[unit], cs2.at[unit], cr2.at[unit], core_dev)

    def x_return(unit):
        return remote(x_out.at[unit], x_in.at[unit], xs2.at[unit], xr2.at[unit], x_dev)

    def z_return(d, chunk):
        return remote(
            z_out.at[d, chunk], z_in.at[d, chunk], zs2.at[d, chunk], zr2.at[d, chunk], (2 * (b - d) + c, head)
        )

    def cross(unit):
        core_return(unit).wait_recv()
        x_out[unit] = (part[unit, c, ox].astype(F32) + core_in[unit, ox].astype(F32)).astype(BF16)
        x_return(unit).start()
        summed[unit] = part[unit, c, x].astype(F32) + core_in[unit, x].astype(F32)

    def land(unit):
        x_return(unit).wait_recv()
        summed[unit] = summed[unit] + x_in[unit].astype(F32)

    def send_back(chunk):
        for slot in range(1, chosen):
            land(2 * slot + chunk)
        for d in reversed(range(1, num_blocks)):
            @pl.when(d <= b)
            def _():
                z_out[d, chunk] = sum(
                    jnp.where(picks[group, slot - 1, b] == d, summed[2 * slot + chunk], 0.0)
                    for slot in range(1, chosen)
                ).astype(BF16)
                z_return(d, chunk).start()

    order = [2 * slot + chunk for chunk in range(2) for slot in range(1, chosen)] + [0, 1]
    for unit in order:
        core_return(unit).start()
    for step, unit in enumerate(order):
        cross(unit)
        if step == 2 * chosen - 3:
            send_back(0)
    send_back(1)
    for chunk in range(2):
        land(chunk)
        for d in range(1, num_blocks):
            @pl.when(b + d < num_blocks)
            def _():
                z_return(d, chunk).wait_recv()
                summed[chunk] = summed[chunk] + z_in[d, chunk].astype(F32)
        at = pl.ds(chunk * part_rows, part_rows)
        grads_out[:, at] = summed[chunk].T

    for d in range(1, num_blocks):
        @pl.when(d <= b)
        def _():
            z_return(d, 0).wait_send()
            z_return(d, 1).wait_send()
    for unit in range(2 * chosen):
        core_return(unit).wait_send()
        x_return(unit).wait_send()


def local(queries, key_states, value_states, block_picks, grad_output):
    rows, half = key_states.shape
    dim = 2 * half
    heads = queries.shape[1] // dim
    num_blocks = lax.axis_size("seq") * rows // BLOCK
    assert BLOCK == 2 * rows
    chosen = block_picks.shape[2] + 1
    keys = chosen * BLOCK
    units = 2 * chosen
    vmem = pl.BlockSpec(memory_space=pltpu.VMEM)
    smem = pl.BlockSpec(memory_space=pltpu.SMEM)
    anywhere = pl.BlockSpec(memory_space=pl.ANY)
    dma = pltpu.SemaphoreType.DMA
    picks = block_picks.transpose(1, 2, 0)
    kv = pl.pallas_call(
        gather,
        out_shape=jax.ShapeDtypeStruct((num_blocks, 2, 2, dim, rows), BF16),
        in_specs=[vmem, vmem],
        out_specs=vmem,
        scratch_shapes=[dma((num_blocks,))] * 4 + [dma((num_blocks, 2))] * 2,
        compiler_params=pltpu.CompilerParams(
            collective_id=0, has_side_effects=True, vmem_limit_bytes=24 * 1024 * 1024
        ),
    )(key_states.T, value_states.T)
    attn, dq, part = pl.pallas_call(
        functools.partial(compute, chosen),
        out_shape=(
            jax.ShapeDtypeStruct(queries.shape, BF16),
            jax.ShapeDtypeStruct(queries.shape, F32),
            jax.ShapeDtypeStruct((units, 2, 2, rows // 2, dim), BF16),
        ),
        in_specs=[smem, vmem, anywhere, anywhere],
        out_specs=(anywhere, anywhere, vmem),
        scratch_shapes=[
            pltpu.VMEM((heads, rows, dim), BF16),
            pltpu.VMEM((heads, rows, dim), BF16),
            pltpu.VMEM((chosen, BLOCK, dim), BF16),
            pltpu.VMEM((chosen, BLOCK, dim), BF16),
            pltpu.VMEM((units, heads, rows, rows), F32),
            pltpu.VMEM((units, heads, rows, rows), F32),
            pltpu.VMEM((keys, heads * rows), BF16),
            pltpu.VMEM((keys, heads * rows), BF16),
            pltpu.VMEM((dim, keys), BF16),
            pltpu.VMEM((dim, keys), BF16),
            pltpu.VMEM((chosen, heads, 1, rows), F32),
            pltpu.VMEM((chosen, heads, 1, rows), F32),
            pltpu.VMEM((chosen, heads, 1, rows), F32),
            pltpu.VMEM((heads * rows, dim), BF16),
            pltpu.VMEM((heads * rows, dim), F32),
            dma((2, heads)),
            dma((2, heads)),
        ],
        compiler_params=pltpu.CompilerParams(vmem_limit_bytes=48 * 1024 * 1024),
        cost_estimate=pl.CostEstimate(
            flops=10 * heads * rows * keys * dim, bytes_accessed=20 * queries.size, transcendentals=heads * rows * keys
        ),
    )(picks, kv, queries, grad_output)
    grads = pl.pallas_call(
        functools.partial(give_back, chosen),
        out_shape=jax.ShapeDtypeStruct((dim, rows), F32),
        in_specs=[smem, vmem],
        out_specs=vmem,
        scratch_shapes=[
            pltpu.VMEM((units, 2, rows // 2, dim), BF16),
            pltpu.VMEM((units, rows // 2, dim), BF16),
            pltpu.VMEM((units, rows // 2, dim), BF16),
            pltpu.VMEM((units, rows // 2, dim), F32),
            pltpu.VMEM((num_blocks, 2, rows // 2, dim), BF16),
            pltpu.VMEM((num_blocks, 2, rows // 2, dim), BF16),
        ]
        + [dma((units,))] * 4
        + [dma((num_blocks, 2))] * 2,
        compiler_params=pltpu.CompilerParams(
            collective_id=1, has_side_effects=True, vmem_limit_bytes=24 * 1024 * 1024
        ),
    )(picks, part)
    return attn, dq, grads[:half].T, grads[half:].T


def solution(mesh):
    return jax.shard_map(
        local,
        mesh=mesh,
        in_specs=(P("seq", "head"), P("seq", "head"), P("seq", "head"), P(), P("seq", "head")),
        out_specs=(P("seq", "head"), P("seq", "head"), P("seq", "head"), P("seq", "head")),
        check_vma=False,
    )
```

```python
import functools

import jax
import jax.numpy as jnp
from jax import lax
from jax.experimental import pallas as pl
from jax.experimental.pallas import tpu as pltpu
from jax.sharding import PartitionSpec as P

BLOCK = 512
NEGATIVE = -1e30
LOG2E = 1.4426950408889634
MESH = pl.DeviceIdType.MESH
F32 = jnp.float32
BF16 = jnp.bfloat16


def dot(a, b, contract):
    return lax.dot_general(a, b, ((contract[:1], contract[1:]), ((), ())), preferred_element_type=F32)


def kernel(
    seq_size, chosen, picks, k_in, v_in, q_hbm, g_hbm, attn_hbm, dq_hbm, grads_out,
    kv, q4, g4, k_low, v_low, ev, dpv, p_low, ds_low, k_t, v_t, top, total, prod, attn_buf, dq_buf,
    part, core_in, x_out, x_in, summed, z_out, z_in,
    in_sem, out_sem, own_sem, zs, zr, xs, xr, cs, cr, cs2, cr2, xs2, xr2, zs2, zr2,
):
    half, rows = k_in.shape
    dim = 2 * half
    heads = q4.shape[0]
    num_blocks = kv.shape[0]
    seq = lax.axis_index("seq")
    head = lax.axis_index("head")
    b, c = seq // 2, seq % 2
    x, group = head % 2, head // 2
    oc, ox = 1 - c, 1 - x
    core_dev = (2 * b + oc, head)
    x_dev = (seq, 2 * group + ox)
    scaling = dim ** (-0.5)
    rate = scaling * LOG2E
    part_rows = rows // 2

    def remote(src, dst, send, recv, dev):
        return pltpu.make_async_remote_copy(
            src_ref=src, dst_ref=dst, send_sem=send, recv_sem=recv, device_id=dev, device_id_type=MESH
        )

    loads = []
    for h in range(heads):
        cols = pl.ds(h * dim, dim)
        loads.append(pltpu.make_async_copy(q_hbm.at[:, cols], q4.at[h], in_sem.at[0, h]))
        loads.append(pltpu.make_async_copy(g_hbm.at[:, cols], g4.at[h], in_sem.at[1, h]))
    own_loads = [
        pltpu.make_async_copy(ref, kv.at[b, c, x, pl.ds(kind * half, half)], own_sem.at[kind])
        for kind, ref in enumerate((k_in, v_in))
    ]
    for load in own_loads + loads:
        load.start()

    barrier = pltpu.get_barrier_semaphore()
    pl.semaphore_signal(barrier, inc=1, device_id=core_dev, device_id_type=MESH)
    pl.semaphore_signal(barrier, inc=1, device_id=x_dev, device_id_type=MESH)
    for d in range(1, num_blocks):
        other = lax.rem(b + d, num_blocks)
        pl.semaphore_signal(barrier, inc=1, device_id=(2 * other + c, head), device_id_type=MESH)
    for load in own_loads:
        load.wait()
    pl.semaphore_wait(barrier, num_blocks + 1)

    def piece(d, row_half, side, part_of):
        return kv.at[b - d, row_half, side, pl.ds(part_of * half, half)]

    def z_gather(d, kind):
        mine = piece(0, c, x, kind)
        return remote(mine, mine, zs.at[d, kind], zr.at[d, kind], (2 * (b + d) + c, head))

    def z_arrival(d, kind):
        there = piece(d, c, x, kind)
        return remote(there, there, zs.at[d, kind], zr.at[d, kind], (2 * (b - d) + c, head))

    def x_gather(d, side, kind):
        there = piece(d, c, side, kind)
        return remote(there, there, xs.at[d, kind], xr.at[d, kind], x_dev)

    def core_gather(d, which, row_half, kind):
        there = piece(d, row_half, x if which == 0 else ox, kind)
        return remote(there, there, cs.at[d, which, kind], cr.at[d, which, kind], core_dev)

    for kind in range(2):
        x_gather(0, x, kind).start()
        for d in reversed(range(1, num_blocks)):
            @pl.when(b + d < num_blocks)
            def _():
                z_gather(d, kind).start()
    for kind in range(2):
        core_gather(0, 0, c, kind).start()

    def forward_z(d, kind):
        @pl.when(d <= b)
        def _():
            z_arrival(d, kind).wait_recv()
            x_gather(d, x, kind).start()
            core_gather(d, 0, c, kind).start()

    def forward_x(d, kind):
        @pl.when(d <= b)
        def _():
            x_gather(d, ox, kind).wait_recv()
            core_gather(d, 1, c, kind).start()

    def settle(d):
        @pl.when(d <= b)
        def _():
            for kind in range(2):
                core_gather(d, 0, oc, kind).wait_recv()
                core_gather(d, 1, oc, kind).wait_recv()

    def tiles(block):
        wide = [jnp.concatenate([kv[block, 0, side], kv[block, 1, side]], axis=1) for side in range(2)]
        keys = jnp.concatenate([wide[0][:half], wide[1][:half]], axis=0)
        values = jnp.concatenate([wide[0][half:], wide[1][half:]], axis=0)
        return keys, values

    def prepare(slot, block):
        key_tile, value_tile = tiles(block)
        for piece in range(4):
            side, chunk = piece % 2, piece // 2
            cut = slice(side * rows + chunk * part_rows, side * rows + (chunk + 1) * part_rows)
            at = pl.ds(pl.multiple_of(slot * BLOCK + piece * part_rows, part_rows), part_rows)
            k_t[:, at] = key_tile[:, cut]
            v_t[:, at] = value_tile[:, cut]
        k_low[slot] = key_tile.astype(F32).T.astype(BF16)
        v_low[slot] = value_tile.astype(F32).T.astype(BF16)

    def first_pass(slot, which, usable, causal):
        for h in which:
            s = dot(k_low[slot], q4[h], (1, 1))
            if causal:
                place = lax.broadcasted_iota(jnp.int32, (BLOCK, rows), 0)
                query = lax.broadcasted_iota(jnp.int32, (BLOCK, rows), 1) + c * rows
                s = jnp.where(place <= query, s, NEGATIVE)
            dp = dot(v_low[slot], g4[h], (1, 1))
            m = jnp.max(s, axis=0, keepdims=True)
            e = jnp.exp2((s - m) * rate)
            for piece in range(4):
                side, chunk = piece % 2, piece // 2
                cut = slice(side * rows + chunk * part_rows, side * rows + (chunk + 1) * part_rows)
                at = slice(side * part_rows, (side + 1) * part_rows)
                ev[2 * slot + chunk, h, at] = e[cut]
                dpv[2 * slot + chunk, h, at] = dp[cut]
            top[slot, h] = m if causal else jnp.where(usable, m, NEGATIVE)
            total[slot, h] = jnp.sum(e, axis=0, keepdims=True)
            prod[slot, h] = jnp.sum(e * dp, axis=0, keepdims=True)

    every = list(range(heads))
    earlier = range(1, num_blocks)
    forward_x(0, 0)
    forward_x(0, 1)
    for kind in range(2):
        for d in earlier:
            forward_z(d, kind)
    for d in earlier:
        forward_x(d, 0)
    for load in loads:
        load.wait()
    settle(0)
    prepare(0, b)
    first_pass(0, every, None, True)
    for d in earlier:
        forward_x(d, 1)
    for d in earlier:
        settle(d)

    @pl.loop(1, chosen)
    def _(slot):
        wanted = b - picks[group, slot - 1, b]
        prepare(slot, jnp.maximum(wanted, 0))
        first_pass(slot, every, wanted >= 0, False)

    for h in every:
        m = top[0, h]
        for slot in range(1, chosen):
            m = jnp.maximum(m, top[slot, h])
        weight = [jnp.exp2((top[slot, h] - m) * rate) for slot in range(chosen)]
        norm = sum(weight[slot] * total[slot, h] for slot in range(chosen))
        share = [w / norm for w in weight]
        for slot in range(chosen):
            top[slot, h] = share[slot]
        total[0, h] = sum(share[slot] * prod[slot, h] for slot in range(chosen))

    def core_return(unit):
        return remote(part.at[unit, oc], core_in.at[unit], cs2.at[unit], cr2.at[unit], core_dev)

    def x_return(unit):
        return remote(x_out.at[unit], x_in.at[unit], xs2.at[unit], xr2.at[unit], x_dev)

    def z_return(d, chunk):
        return remote(
            z_out.at[d, chunk], z_in.at[d, chunk], zs2.at[d, chunk], zr2.at[d, chunk], (2 * (b - d) + c, head)
        )

    def second_pass(unit):
        slot = unit // 2
        at = pl.ds(pl.multiple_of(unit * 2 * part_rows, 2 * part_rows), 2 * part_rows)
        grad_k = grad_v = 0.0
        for h in every:
            cols = slice(h * rows, (h + 1) * rows)
            probs = ev[unit, h] * top[slot, h]
            low = probs.astype(BF16)
            ds = (probs * (dpv[unit, h] - total[0, h])).astype(BF16)
            p_low[at, cols] = low
            ds_low[at, cols] = ds
            grad_v += dot(low, g4[h], (1, 0))
            grad_k += dot(ds, q4[h], (1, 0))
        grad_k = grad_k * scaling
        lanes = lax.broadcasted_iota(jnp.int32, grad_k.shape, 1) < half
        left = jnp.where(lanes, grad_k, pltpu.roll(grad_v, half, 1)).astype(BF16)
        right = jnp.where(lanes, pltpu.roll(grad_k, half, 1), grad_v).astype(BF16)
        for side in range(2):
            cut = slice(side * part_rows, (side + 1) * part_rows)
            part[unit, side, 0] = left[cut]
            part[unit, side, 1] = right[cut]
        core_return(unit).start()

    def cross(unit):
        core_return(unit).wait_recv()
        x_out[unit] = (part[unit, c, ox].astype(F32) + core_in[unit, ox].astype(F32)).astype(BF16)
        x_return(unit).start()
        summed[unit] = part[unit, c, x].astype(F32) + core_in[unit, x].astype(F32)

    def land(unit):
        x_return(unit).wait_recv()
        summed[unit] = summed[unit] + x_in[unit].astype(F32)

    def send_back(chunk):
        for slot in range(1, chosen):
            land(2 * slot + chunk)
        for d in reversed(range(1, num_blocks)):
            @pl.when(d <= b)
            def _():
                z_out[d, chunk] = sum(
                    jnp.where(picks[group, slot - 1, b] == d, summed[2 * slot + chunk], 0.0)
                    for slot in range(1, chosen)
                ).astype(BF16)
                z_return(d, chunk).start()

    others = chosen - 1

    def unit_of(step):
        tail = step // (2 * others)
        slot = (1 - tail) * (1 + step % others)
        return 2 * slot + (1 - tail) * (step // others) + tail * (step - 2 * others)

    @pl.loop(0, 2 * chosen)
    def _(step):
        second_pass(unit_of(step))

        @pl.when(step > 0)
        def _():
            cross(unit_of(step - 1))

        @pl.when(step == 2 * others - 1)
        def _():
            send_back(0)

    send_back(1)
    cross(1)

    attn_buf[...] = dot(v_t[...], p_low[...], (1, 0)).T.astype(BF16)
    dq_buf[...] = (dot(k_t[...], ds_low[...], (1, 0)) * scaling).T
    stores = []
    for h in range(heads):
        at, cols = pl.ds(h * rows, rows), pl.ds(h * dim, dim)
        stores.append(pltpu.make_async_copy(attn_buf.at[at], attn_hbm.at[:, cols], out_sem.at[0, h]))
        stores.append(pltpu.make_async_copy(dq_buf.at[at], dq_hbm.at[:, cols], out_sem.at[1, h]))
        stores[-2].start()
        stores[-1].start()

    for chunk in range(2):
        land(chunk)
        for d in range(1, num_blocks):
            @pl.when(b + d < num_blocks)
            def _():
                z_return(d, chunk).wait_recv()
                summed[chunk] = summed[chunk] + z_in[d, chunk].astype(F32)
        at = pl.ds(chunk * part_rows, part_rows)
        grads_out[:, at] = summed[chunk].T

    for store in stores:
        store.wait()
    for d in range(num_blocks):
        @pl.when(d <= b)
        def _():
            for kind in range(2):
                x_gather(d, x, kind).wait_send()
                core_gather(d, 0, c, kind).wait_send()
                core_gather(d, 1, c, kind).wait_send()
    for d in range(1, num_blocks):
        @pl.when(b + d < num_blocks)
        def _():
            z_gather(d, 0).wait_send()
            z_gather(d, 1).wait_send()
    for d in range(1, num_blocks):
        @pl.when(d <= b)
        def _():
            z_return(d, 0).wait_send()
            z_return(d, 1).wait_send()
    for unit in range(2 * chosen):
        core_return(unit).wait_send()
        x_return(unit).wait_send()


def settle_outputs(attn, dq, grads, attn_out, dq_out, dk_out, dv_out, attn_buf, dq_buf, grads_buf, sem):
    rows, half = attn.shape[0], dk_out.shape[0]
    cut = rows // 2
    moves = []
    for i in range(2):
        at = pl.ds(i * cut, cut)
        moves.append((dq.at[at], dq_buf.at[at], dq_out.at[at]))
        moves.append((attn.at[at], attn_buf.at[at], attn_out.at[at]))
    for i, out in enumerate((dk_out, dv_out)):
        at = pl.ds(i * half, half)
        moves.append((grads.at[at], grads_buf.at[at], out))
    arrive = [pltpu.make_async_copy(src, mid, sem.at[0, i]) for i, (src, mid, _) in enumerate(moves)]
    leave = [pltpu.make_async_copy(mid, dst, sem.at[1, i]) for i, (_, mid, dst) in enumerate(moves)]
    for copy in arrive:
        copy.start()
    for first, then in zip(arrive, leave):
        first.wait()
        then.start()
    for copy in leave:
        copy.wait()


def local(queries, key_states, value_states, block_picks, grad_output):
    rows, half = key_states.shape
    dim = 2 * half
    heads = queries.shape[1] // dim
    seq_size = lax.axis_size("seq")
    num_blocks = seq_size * rows // BLOCK
    assert BLOCK == 2 * rows
    chosen = block_picks.shape[2] + 1
    keys = chosen * BLOCK
    vmem = pl.BlockSpec(memory_space=pltpu.VMEM)
    anywhere = pl.BlockSpec(memory_space=pl.ANY)
    dma = pltpu.SemaphoreType.DMA
    attn, dq, grads = pl.pallas_call(
        functools.partial(kernel, seq_size, chosen),
        out_shape=(
            jax.ShapeDtypeStruct(queries.shape, BF16),
            jax.ShapeDtypeStruct(queries.shape, F32),
            jax.ShapeDtypeStruct((dim, rows), F32),
        ),
        in_specs=[pl.BlockSpec(memory_space=pltpu.SMEM)] + [anywhere] * 4,
        out_specs=(anywhere, anywhere, vmem),
        scratch_shapes=[
            pltpu.VMEM((num_blocks, 2, 2, dim, rows), BF16),
            pltpu.VMEM((heads, rows, dim), BF16),
            pltpu.VMEM((heads, rows, dim), BF16),
            pltpu.VMEM((chosen, BLOCK, dim), BF16),
            pltpu.VMEM((chosen, BLOCK, dim), BF16),
            pltpu.VMEM((2 * chosen, heads, rows, rows), F32),
            pltpu.VMEM((2 * chosen, heads, rows, rows), F32),
            pltpu.VMEM((keys, heads * rows), BF16),
            pltpu.VMEM((keys, heads * rows), BF16),
            pltpu.VMEM((dim, keys), BF16),
            pltpu.VMEM((dim, keys), BF16),
            pltpu.VMEM((chosen, heads, 1, rows), F32),
            pltpu.VMEM((chosen, heads, 1, rows), F32),
            pltpu.VMEM((chosen, heads, 1, rows), F32),
            pltpu.VMEM((heads * rows, dim), BF16),
            pltpu.VMEM((heads * rows, dim), F32),
            pltpu.VMEM((2 * chosen, 2, 2, rows // 2, dim), BF16),
            pltpu.VMEM((2 * chosen, 2, rows // 2, dim), BF16),
            pltpu.VMEM((2 * chosen, rows // 2, dim), BF16),
            pltpu.VMEM((2 * chosen, rows // 2, dim), BF16),
            pltpu.VMEM((2 * chosen, rows // 2, dim), F32),
            pltpu.VMEM((num_blocks, 2, rows // 2, dim), BF16),
            pltpu.VMEM((num_blocks, 2, rows // 2, dim), BF16),
            dma((2, heads)),
            dma((2, heads)),
            dma((2,)),
            dma((num_blocks, 2)),
            dma((num_blocks, 2)),
            dma((num_blocks, 2)),
            dma((num_blocks, 2)),
            dma((num_blocks, 2, 2)),
            dma((num_blocks, 2, 2)),
            dma((2 * chosen,)),
            dma((2 * chosen,)),
            dma((2 * chosen,)),
            dma((2 * chosen,)),
            dma((num_blocks, 2)),
            dma((num_blocks, 2)),
        ],
        compiler_params=pltpu.CompilerParams(
            collective_id=0, has_side_effects=True, vmem_limit_bytes=56 * 1024 * 1024
        ),
        cost_estimate=pl.CostEstimate(
            flops=10 * heads * rows * keys * dim, bytes_accessed=4 * queries.size * 4, transcendentals=heads * rows * keys
        ),
    )(block_picks.transpose(1, 2, 0), key_states.T, value_states.T, queries, grad_output)
    attn, dq, dk, dv = pl.pallas_call(
        settle_outputs,
        out_shape=(
            jax.ShapeDtypeStruct(attn.shape, attn.dtype),
            jax.ShapeDtypeStruct(dq.shape, dq.dtype),
            jax.ShapeDtypeStruct((half, rows), F32),
            jax.ShapeDtypeStruct((half, rows), F32),
        ),
        in_specs=[anywhere] * 3,
        out_specs=(anywhere,) * 4,
        scratch_shapes=[
            pltpu.VMEM(attn.shape, attn.dtype),
            pltpu.VMEM(dq.shape, dq.dtype),
            pltpu.VMEM(grads.shape, grads.dtype),
            dma((2, 6)),
        ],
        cost_estimate=pl.CostEstimate(flops=0, bytes_accessed=2 * 7 * queries.size, transcendentals=0),
    )(attn, dq, grads)
    return attn, dq, dk.T, dv.T


def solution(mesh):
    return jax.shard_map(
        local,
        mesh=mesh,
        in_specs=(P("seq", "head"), P("seq", "head"), P("seq", "head"), P(), P("seq", "head")),
        out_specs=(P("seq", "head"), P("seq", "head"), P("seq", "head"), P("seq", "head")),
        check_vma=False,
    )
```

```python
import functools

import jax
import jax.numpy as jnp
from jax import lax
from jax.experimental import pallas as pl
from jax.experimental.pallas import tpu as pltpu
from jax.sharding import PartitionSpec as P

BLOCK = 512
NEGATIVE = -1e30
LOG2E = 1.4426950408889634
MESH = pl.DeviceIdType.MESH
F32 = jnp.float32
BF16 = jnp.bfloat16


def dot(a, b, contract):
    return lax.dot_general(a, b, ((contract[:1], contract[1:]), ((), ())), preferred_element_type=F32)


def kernel(
    seq_size, chosen, picks, k_in, v_in, q_hbm, g_hbm, attn_hbm, dq_hbm, grads_out,
    kv, q4, g4, k_low, v_low, ev, dpv, p_low, ds_low, k_t, v_t, top, total, prod, attn_buf, dq_buf,
    part, core_in, x_out, x_in, summed, z_out, z_in,
    in_sem, out_sem, own_sem, zs, zr, xs, xr, cs, cr, cs2, cr2, xs2, xr2, zs2, zr2,
):
    half, rows = k_in.shape
    dim = 2 * half
    heads = q4.shape[0]
    num_blocks = kv.shape[0]
    seq = lax.axis_index("seq")
    head = lax.axis_index("head")
    b, c = seq // 2, seq % 2
    x, group = head % 2, head // 2
    oc, ox = 1 - c, 1 - x
    core_dev = (2 * b + oc, head)
    x_dev = (seq, 2 * group + ox)
    scaling = dim ** (-0.5)
    rate = scaling * LOG2E
    part_rows = rows // 2

    def remote(src, dst, send, recv, dev):
        return pltpu.make_async_remote_copy(
            src_ref=src, dst_ref=dst, send_sem=send, recv_sem=recv, device_id=dev, device_id_type=MESH
        )

    loads = []
    for h in range(heads):
        cols = pl.ds(h * dim, dim)
        loads.append(pltpu.make_async_copy(q_hbm.at[:, cols], q4.at[h], in_sem.at[0, h]))
        loads.append(pltpu.make_async_copy(g_hbm.at[:, cols], g4.at[h], in_sem.at[1, h]))
    own_loads = [
        pltpu.make_async_copy(ref, kv.at[b, c, x, pl.ds(kind * half, half)], own_sem.at[kind])
        for kind, ref in enumerate((k_in, v_in))
    ]
    for load in own_loads + loads:
        load.start()

    barrier = pltpu.get_barrier_semaphore()
    pl.semaphore_signal(barrier, inc=1, device_id=core_dev, device_id_type=MESH)
    pl.semaphore_signal(barrier, inc=1, device_id=x_dev, device_id_type=MESH)
    for d in range(1, num_blocks):
        other = lax.rem(b + d, num_blocks)
        pl.semaphore_signal(barrier, inc=1, device_id=(2 * other + c, head), device_id_type=MESH)
    for load in own_loads:
        load.wait()
    pl.semaphore_wait(barrier, num_blocks + 1)

    def piece(d, row_half, side, part_of):
        return kv.at[b - d, row_half, side, pl.ds(part_of * half, half)]

    def z_gather(d, kind):
        mine = piece(0, c, x, kind)
        return remote(mine, mine, zs.at[d, kind], zr.at[d, kind], (2 * (b + d) + c, head))

    def z_arrival(d, kind):
        there = piece(d, c, x, kind)
        return remote(there, there, zs.at[d, kind], zr.at[d, kind], (2 * (b - d) + c, head))

    def x_gather(d, side, kind):
        there = piece(d, c, side, kind)
        return remote(there, there, xs.at[d, kind], xr.at[d, kind], x_dev)

    def core_gather(d, which, row_half, kind):
        there = piece(d, row_half, x if which == 0 else ox, kind)
        return remote(there, there, cs.at[d, which, kind], cr.at[d, which, kind], core_dev)

    for kind in range(2):
        x_gather(0, x, kind).start()
        for d in reversed(range(1, num_blocks)):
            @pl.when(b + d < num_blocks)
            def _():
                z_gather(d, kind).start()
    for kind in range(2):
        core_gather(0, 0, c, kind).start()

    def forward_z(d, kind):
        @pl.when(d <= b)
        def _():
            z_arrival(d, kind).wait_recv()
            x_gather(d, x, kind).start()
            core_gather(d, 0, c, kind).start()

    def forward_x(d, kind):
        @pl.when(d <= b)
        def _():
            x_gather(d, ox, kind).wait_recv()
            core_gather(d, 1, c, kind).start()

    def settle(d):
        @pl.when(d <= b)
        def _():
            for kind in range(2):
                core_gather(d, 0, oc, kind).wait_recv()
                core_gather(d, 1, oc, kind).wait_recv()

    def tiles(block):
        wide = [jnp.concatenate([kv[block, 0, side], kv[block, 1, side]], axis=1) for side in range(2)]
        keys = jnp.concatenate([wide[0][:half], wide[1][:half]], axis=0)
        values = jnp.concatenate([wide[0][half:], wide[1][half:]], axis=0)
        return keys, values

    def prepare(slot, block):
        key_tile, value_tile = tiles(block)
        for piece in range(4):
            side, chunk = piece % 2, piece // 2
            cut = slice(side * rows + chunk * part_rows, side * rows + (chunk + 1) * part_rows)
            at = pl.ds(pl.multiple_of(slot * BLOCK + piece * part_rows, part_rows), part_rows)
            k_t[:, at] = key_tile[:, cut]
            v_t[:, at] = value_tile[:, cut]
        k_low[slot] = key_tile.astype(F32).T.astype(BF16)
        v_low[slot] = value_tile.astype(F32).T.astype(BF16)

    def first_pass(slot, which, usable, causal):
        for h in which:
            s = dot(k_low[slot], q4[h], (1, 1))
            if causal:
                place = lax.broadcasted_iota(jnp.int32, (BLOCK, rows), 0)
                query = lax.broadcasted_iota(jnp.int32, (BLOCK, rows), 1) + c * rows
                s = jnp.where(place <= query, s, NEGATIVE)
            dp = dot(v_low[slot], g4[h], (1, 1))
            m = jnp.max(s, axis=0, keepdims=True)
            e = jnp.exp2((s - m) * rate)
            for piece in range(4):
                side, chunk = piece % 2, piece // 2
                cut = slice(side * rows + chunk * part_rows, side * rows + (chunk + 1) * part_rows)
                at = slice(side * part_rows, (side + 1) * part_rows)
                ev[2 * slot + chunk, h, at] = e[cut]
                dpv[2 * slot + chunk, h, at] = dp[cut]
            top[slot, h] = m if causal else jnp.where(usable, m, NEGATIVE)
            total[slot, h] = jnp.sum(e, axis=0, keepdims=True)
            prod[slot, h] = jnp.sum(e * dp, axis=0, keepdims=True)

    every = list(range(heads))
    earlier = range(1, num_blocks)
    forward_x(0, 0)
    forward_x(0, 1)
    for kind in range(2):
        for d in earlier:
            forward_z(d, kind)
    for d in earlier:
        forward_x(d, 0)
    for load in loads:
        load.wait()
    settle(0)
    prepare(0, b)
    first_pass(0, every, None, True)
    for d in earlier:
        forward_x(d, 1)
    for d in earlier:
        settle(d)

    @pl.loop(1, chosen)
    def _(slot):
        wanted = b - picks[group, slot - 1, b]
        prepare(slot, jnp.maximum(wanted, 0))
        first_pass(slot, every, wanted >= 0, False)

    for h in every:
        m = top[0, h]
        for slot in range(1, chosen):
            m = jnp.maximum(m, top[slot, h])
        weight = [jnp.exp2((top[slot, h] - m) * rate) for slot in range(chosen)]
        norm = sum(weight[slot] * total[slot, h] for slot in range(chosen))
        share = [w / norm for w in weight]
        for slot in range(chosen):
            top[slot, h] = share[slot]
        total[0, h] = sum(share[slot] * prod[slot, h] for slot in range(chosen))

    def core_return(unit):
        return remote(part.at[unit, oc], core_in.at[unit], cs2.at[unit], cr2.at[unit], core_dev)

    def x_return(unit):
        return remote(x_out.at[unit], x_in.at[unit], xs2.at[unit], xr2.at[unit], x_dev)

    def z_return(d, chunk):
        return remote(
            z_out.at[d, chunk], z_in.at[d, chunk], zs2.at[d, chunk], zr2.at[d, chunk], (2 * (b - d) + c, head)
        )

    def second_pass(unit):
        slot = unit // 2
        at = pl.ds(pl.multiple_of(unit * 2 * part_rows, 2 * part_rows), 2 * part_rows)
        grad_k = grad_v = 0.0
        for h in every:
            cols = slice(h * rows, (h + 1) * rows)
            probs = ev[unit, h] * top[slot, h]
            low = probs.astype(BF16)
            ds = (probs * (dpv[unit, h] - total[0, h])).astype(BF16)
            p_low[at, cols] = low
            ds_low[at, cols] = ds
            grad_v += dot(low, g4[h], (1, 0))
            grad_k += dot(ds, q4[h], (1, 0))
        grad_k = grad_k * scaling
        lanes = lax.broadcasted_iota(jnp.int32, grad_k.shape, 1) < half
        left = jnp.where(lanes, grad_k, pltpu.roll(grad_v, half, 1)).astype(BF16)
        right = jnp.where(lanes, pltpu.roll(grad_k, half, 1), grad_v).astype(BF16)
        for side in range(2):
            cut = slice(side * part_rows, (side + 1) * part_rows)
            part[unit, side, 0] = left[cut]
            part[unit, side, 1] = right[cut]
        core_return(unit).start()

    def cross(unit):
        core_return(unit).wait_recv()
        x_out[unit] = (part[unit, c, ox].astype(F32) + core_in[unit, ox].astype(F32)).astype(BF16)
        x_return(unit).start()
        summed[unit] = part[unit, c, x].astype(F32) + core_in[unit, x].astype(F32)

    def land(unit):
        x_return(unit).wait_recv()
        summed[unit] = summed[unit] + x_in[unit].astype(F32)

    def send_back(chunk):
        for slot in range(1, chosen):
            land(2 * slot + chunk)
        for d in reversed(range(1, num_blocks)):
            @pl.when(d <= b)
            def _():
                z_out[d, chunk] = sum(
                    jnp.where(picks[group, slot - 1, b] == d, summed[2 * slot + chunk], 0.0)
                    for slot in range(1, chosen)
                ).astype(BF16)
                z_return(d, chunk).start()

    others = chosen - 1

    def unit_of(step):
        tail = step // (2 * others)
        slot = (1 - tail) * (1 + step % others)
        return 2 * slot + (1 - tail) * (step // others) + tail * (step - 2 * others)

    @pl.loop(0, 2 * chosen)
    def _(step):
        second_pass(unit_of(step))

        @pl.when(step > 1)
        def _():
            cross(unit_of(step - 2))

        @pl.when(step == 2 * others)
        def _():
            send_back(0)

    cross(0)
    send_back(1)
    cross(1)

    attn_buf[...] = dot(v_t[...], p_low[...], (1, 0)).T.astype(BF16)
    dq_buf[...] = (dot(k_t[...], ds_low[...], (1, 0)) * scaling).T
    stores = []
    for h in range(heads):
        at, cols = pl.ds(h * rows, rows), pl.ds(h * dim, dim)
        stores.append(pltpu.make_async_copy(attn_buf.at[at], attn_hbm.at[:, cols], out_sem.at[0, h]))
        stores.append(pltpu.make_async_copy(dq_buf.at[at], dq_hbm.at[:, cols], out_sem.at[1, h]))
        stores[-2].start()
        stores[-1].start()

    for chunk in range(2):
        land(chunk)
        for d in range(1, num_blocks):
            @pl.when(b + d < num_blocks)
            def _():
                z_return(d, chunk).wait_recv()
                summed[chunk] = summed[chunk] + z_in[d, chunk].astype(F32)
        at = pl.ds(chunk * part_rows, part_rows)
        grads_out[:, at] = summed[chunk].T

    for store in stores:
        store.wait()
    for d in range(num_blocks):
        @pl.when(d <= b)
        def _():
            for kind in range(2):
                x_gather(d, x, kind).wait_send()
                core_gather(d, 0, c, kind).wait_send()
                core_gather(d, 1, c, kind).wait_send()
    for d in range(1, num_blocks):
        @pl.when(b + d < num_blocks)
        def _():
            z_gather(d, 0).wait_send()
            z_gather(d, 1).wait_send()
    for d in range(1, num_blocks):
        @pl.when(d <= b)
        def _():
            z_return(d, 0).wait_send()
            z_return(d, 1).wait_send()
    for unit in range(2 * chosen):
        core_return(unit).wait_send()
        x_return(unit).wait_send()


def settle_outputs(attn, dq, grads, attn_out, dq_out, dk_out, dv_out, attn_buf, dq_buf, grads_buf, sem):
    rows, half = attn.shape[0], dk_out.shape[0]
    cut = rows // 2
    moves = []
    for i in range(2):
        at = pl.ds(i * cut, cut)
        moves.append((dq.at[at], dq_buf.at[at], dq_out.at[at]))
        moves.append((attn.at[at], attn_buf.at[at], attn_out.at[at]))
    for i, out in enumerate((dk_out, dv_out)):
        at = pl.ds(i * half, half)
        moves.append((grads.at[at], grads_buf.at[at], out))
    arrive = [pltpu.make_async_copy(src, mid, sem.at[0, i]) for i, (src, mid, _) in enumerate(moves)]
    leave = [pltpu.make_async_copy(mid, dst, sem.at[1, i]) for i, (_, mid, dst) in enumerate(moves)]
    for copy in arrive:
        copy.start()
    for first, then in zip(arrive, leave):
        first.wait()
        then.start()
    for copy in leave:
        copy.wait()


def local(queries, key_states, value_states, block_picks, grad_output):
    rows, half = key_states.shape
    dim = 2 * half
    heads = queries.shape[1] // dim
    seq_size = lax.axis_size("seq")
    num_blocks = seq_size * rows // BLOCK
    assert BLOCK == 2 * rows
    chosen = block_picks.shape[2] + 1
    keys = chosen * BLOCK
    vmem = pl.BlockSpec(memory_space=pltpu.VMEM)
    anywhere = pl.BlockSpec(memory_space=pl.ANY)
    dma = pltpu.SemaphoreType.DMA
    attn, dq, grads = pl.pallas_call(
        functools.partial(kernel, seq_size, chosen),
        out_shape=(
            jax.ShapeDtypeStruct(queries.shape, BF16),
            jax.ShapeDtypeStruct(queries.shape, F32),
            jax.ShapeDtypeStruct((dim, rows), F32),
        ),
        in_specs=[pl.BlockSpec(memory_space=pltpu.SMEM)] + [anywhere] * 4,
        out_specs=(anywhere, anywhere, vmem),
        scratch_shapes=[
            pltpu.VMEM((num_blocks, 2, 2, dim, rows), BF16),
            pltpu.VMEM((heads, rows, dim), BF16),
            pltpu.VMEM((heads, rows, dim), BF16),
            pltpu.VMEM((chosen, BLOCK, dim), BF16),
            pltpu.VMEM((chosen, BLOCK, dim), BF16),
            pltpu.VMEM((2 * chosen, heads, rows, rows), F32),
            pltpu.VMEM((2 * chosen, heads, rows, rows), F32),
            pltpu.VMEM((keys, heads * rows), BF16),
            pltpu.VMEM((keys, heads * rows), BF16),
            pltpu.VMEM((dim, keys), BF16),
            pltpu.VMEM((dim, keys), BF16),
            pltpu.VMEM((chosen, heads, 1, rows), F32),
            pltpu.VMEM((chosen, heads, 1, rows), F32),
            pltpu.VMEM((chosen, heads, 1, rows), F32),
            pltpu.VMEM((heads * rows, dim), BF16),
            pltpu.VMEM((heads * rows, dim), F32),
            pltpu.VMEM((2 * chosen, 2, 2, rows // 2, dim), BF16),
            pltpu.VMEM((2 * chosen, 2, rows // 2, dim), BF16),
            pltpu.VMEM((2 * chosen, rows // 2, dim), BF16),
            pltpu.VMEM((2 * chosen, rows // 2, dim), BF16),
            pltpu.VMEM((2 * chosen, rows // 2, dim), F32),
            pltpu.VMEM((num_blocks, 2, rows // 2, dim), BF16),
            pltpu.VMEM((num_blocks, 2, rows // 2, dim), BF16),
            dma((2, heads)),
            dma((2, heads)),
            dma((2,)),
            dma((num_blocks, 2)),
            dma((num_blocks, 2)),
            dma((num_blocks, 2)),
            dma((num_blocks, 2)),
            dma((num_blocks, 2, 2)),
            dma((num_blocks, 2, 2)),
            dma((2 * chosen,)),
            dma((2 * chosen,)),
            dma((2 * chosen,)),
            dma((2 * chosen,)),
            dma((num_blocks, 2)),
            dma((num_blocks, 2)),
        ],
        compiler_params=pltpu.CompilerParams(
            collective_id=0, has_side_effects=True, vmem_limit_bytes=56 * 1024 * 1024
        ),
        cost_estimate=pl.CostEstimate(
            flops=10 * heads * rows * keys * dim, bytes_accessed=4 * queries.size * 4, transcendentals=heads * rows * keys
        ),
    )(block_picks.transpose(1, 2, 0), key_states.T, value_states.T, queries, grad_output)
    attn, dq, dk, dv = pl.pallas_call(
        settle_outputs,
        out_shape=(
            jax.ShapeDtypeStruct(attn.shape, attn.dtype),
            jax.ShapeDtypeStruct(dq.shape, dq.dtype),
            jax.ShapeDtypeStruct((half, rows), F32),
            jax.ShapeDtypeStruct((half, rows), F32),
        ),
        in_specs=[anywhere] * 3,
        out_specs=(anywhere,) * 4,
        scratch_shapes=[
            pltpu.VMEM(attn.shape, attn.dtype),
            pltpu.VMEM(dq.shape, dq.dtype),
            pltpu.VMEM(grads.shape, grads.dtype),
            dma((2, 6)),
        ],
        cost_estimate=pl.CostEstimate(flops=0, bytes_accessed=2 * 7 * queries.size, transcendentals=0),
    )(attn, dq, grads)
    return attn, dq, dk.T, dv.T


def solution(mesh):
    return jax.shard_map(
        local,
        mesh=mesh,
        in_specs=(P("seq", "head"), P("seq", "head"), P("seq", "head"), P(), P("seq", "head")),
        out_specs=(P("seq", "head"), P("seq", "head"), P("seq", "head"), P("seq", "head")),
        check_vma=False,
    )
```
